128 devices in a mesh: row: 16 (over y, z_hi, core), col: 8 (over z_lo, x).
Axes of the slice: x: 4, y: 4, z: 4 (z_hi: 2, z_lo: 2; z = z_hi * 2 + z_lo), core: 2. Of those that a mesh axis runs over, the one named last changes fastest.
Arguments:
- fine_input: bfloat16 [1, 512, 1024, 256], P(None, 'row', 'col'), may hold values from -6 to 6
- coarse_feat: bfloat16 [1, 128, 256, 256], P(None, ('row', 'col')), may hold values from -6 to 6
- conv_weight: bfloat16 [3, 3, 256, 256], replicated, may hold values from -0.125 to 0.125
- step_scale: float32 [1000, 256], replicated, may hold values from 0.5 to 2
- timesteps: int32 [1], replicated, may hold values from 0 to 999
- cotangent: bfloat16 [1, 512, 1024, 256], P(None, 'row', 'col'), may hold values from -6 to 6
Outputs:
- grad_fine: bfloat16 [1, 512, 1024, 256], P(None, 'row', 'col')
- grad_coarse: bfloat16 [1, 128, 256, 256], P(None, ('row', 'col'))
- grad_weight: float32 [3, 3, 256, 256], replicated
The draws below stay inside these ranges and needn't reach their ends.
All inputs are finite; a program needn't handle non-finite values.
Results may differ from the reference program's by a relative error of at most 0.013.
Values may be sent and summed in bfloat16 or wider, within the bound.
A program may use at most 128 MiB of HBM per device.

```python
import math
import jax
import jax.numpy as jnp
from jax import lax

C = 256
TSTEPS = 1000
FR = 1
HF = 512
WF = 1024
HC = 128
WC = 256


def shard_levels(rng, extent, split, smallest, top_value):
    def one(axis_at, blocks):
        heights = jax.random.uniform(jax.random.fold_in(jax.random.fold_in(rng, 6), axis_at), (blocks,), jnp.float32, smallest / len(split), top_value / len(split))
        return jnp.repeat(jnp.exp(heights), extent[axis_at] // blocks).reshape((-1,) + (1,) * (len(extent) - axis_at - 1))

    loudness = one(*split[0])
    for cut in split[1:]:
        loudness = loudness * one(*cut)
    return loudness


def centred(own_key, extent, width, most, cuts=(), kind=jnp.bfloat16):
    entries = width * jax.random.normal(own_key, extent, jnp.float32)
    if cuts:
        entries = entries * shard_levels(own_key, extent, cuts, -0.22, 0.18)
    return jnp.clip(entries, -most, most).astype(kind)


def setup_inputs(seed: int = 0) -> dict:
    arg_keys = jax.random.split(jax.random.key(seed), 7)
    fine_input = centred(arg_keys[0], (FR, HF, WF, C), 1.0, 6.0, ((1, 16), (2, 8)))
    coarse_feat = centred(arg_keys[1], (FR, HC, WC, C), 1.0, 6.0, ((1, 128),))
    conv_weight = centred(arg_keys[2], (3, 3, C, C), (9 * C) ** -0.5, 0.125)
    step_scale = jnp.clip(jnp.exp(jax.random.uniform(arg_keys[3], (TSTEPS, C), jnp.float32, math.log(0.5), math.log(2.0))), 0.5, 2.0)
    timesteps = jax.random.randint(arg_keys[4], (FR,), 0, TSTEPS).astype(jnp.int32)
    cotangent = centred(arg_keys[5], (FR, HF, WF, C), 1.0, 6.0, ((1, 16), (2, 8)))
    return dict(fine_input=fine_input, coarse_feat=coarse_feat, conv_weight=conv_weight, step_scale=step_scale, timesteps=timesteps, cotangent=cotangent)


def reference(fine_input, coarse_feat, conv_weight, step_scale, timesteps, cotangent):
    upper = jnp.repeat(jnp.repeat(coarse_feat.astype(jnp.float32), 4, axis=1), 4, axis=2)
    hidden = fine_input.astype(jnp.float32) + upper
    sig = jax.nn.sigmoid(hidden)
    act = (hidden * sig).astype(jnp.bfloat16)
    onehot = (timesteps[:, None] == jnp.arange(TSTEPS, dtype=jnp.int32)[None, :]).astype(jnp.float32)
    picked = jnp.dot(onehot, step_scale, precision=lax.Precision.HIGHEST)
    dpre = (cotangent.astype(jnp.float32) * picked[:, None, None, :]).astype(jnp.bfloat16)
    pad_act = jnp.pad(act, ((0, 0), (1, 1), (1, 1), (0, 0)))
    pad_grad = jnp.pad(dpre, ((0, 0), (1, 1), (1, 1), (0, 0)))
    flat_grad = dpre.reshape(-1, C)
    rows_w = []
    dact = jnp.zeros((FR * HF * WF, C), jnp.float32)
    for i in range(3):
        taps = []
        for j in range(3):
            window = pad_act[:, i:i + HF, j:j + WF, :].reshape(-1, C)
            taps.append(lax.dot_general(window, flat_grad, (((0,), (0,)), ((), ())), preferred_element_type=jnp.float32))
            moved = pad_grad[:, 2 - i:2 - i + HF, 2 - j:2 - j + WF, :].reshape(-1, C)
            dact = dact + lax.dot_general(moved, conv_weight[i, j], (((1,), (1,)), ((), ())), preferred_element_type=jnp.float32)
        rows_w.append(jnp.stack(taps))
    grad_weight = jnp.stack(rows_w) / jnp.sqrt(jnp.float32(FR * HF * WF))
    dhidden = dact.reshape(FR, HF, WF, C) * sig * (1.0 + hidden * (1.0 - sig))
    grad_fine = dhidden.astype(jnp.bfloat16)
    grad_coarse = dhidden.reshape(FR, HC, 4, WC, 4, C).sum(axis=(2, 4)).astype(jnp.bfloat16)
    return (grad_fine, grad_coarse, grad_weight)
```

```python
import functools
import math

import jax
import jax.numpy as jnp
from jax import lax
from jax.experimental import pallas as pl
from jax.experimental.pallas import tpu as pltpu
from jax.sharding import PartitionSpec as P

MESH = pl.DeviceIdType.MESH
BF = jnp.bfloat16
F32 = jnp.float32
TN = (((0,), (0,)), ((), ()))
ROWS, COLS, C = 32, 128, 256
PIX = ROWS * COLS
GRID = (16, 8)
STRIPS = 8
PIECE = C // 8


def place(x, y, z, k):
    return (y * 4 + (z // 2) * 2 + k, (z % 2) * 4 + x)


def other(axis, d, flip, x, y, z, k):
    at = [x, y, z]
    at[axis] = (at[axis] + d) % 4
    return place(*at, (k + flip) % 2)


def fused_kernel(
    ts_ref, ss_hbm, fine_hbm, coarse_hbm, w_hbm, cot_hbm,
    gf_ref, gc_ref, gw_ref,
    ss, cot, fine, w, wcat, dcat, act, slope,
    edge32, edge, got_edge, got_row, got_corner, got_coarse, up, patch,
    pool, got_pool, part, stack1, stack2, stack3, whole, pooled_rows,
    load_sem, out_sem, in_sem, pool_out, pool_in, ar_out, ar_in,
):
    row, col = lax.axis_index("row"), lax.axis_index("col")
    y, z, k, x = row // 4, ((row // 2) % 2) * 2 + col // 4, row % 2, col % 4
    here = (x, y, z, k)

    loads = [
        pltpu.make_async_copy(cot_hbm, cot, load_sem.at[0]),
        pltpu.make_async_copy(ss_hbm, ss, load_sem.at[1]),
        pltpu.make_async_copy(w_hbm, w, load_sem.at[2]),
        pltpu.make_async_copy(fine_hbm, fine, load_sem.at[3]),
        pltpu.make_async_copy(
            coarse_hbm.at[pl.ds(col * 32, 32)], got_coarse.at[col], load_sem.at[4]
        ),
    ]

    partners = [(row, (col + d) % 8) for d in range(1, 8)]
    partners += [((row + 1) % 16, col), ((row + 15) % 16, col)]
    partners += [((row + a) % 16, (col + b) % 8) for a in (1, 15) for b in (1, 7)]
    for axis in range(3):
        for d in range(1, 4):
            if axis:
                partners.append(other(axis, d, 0, *here))
            partners.append(other(axis, d, 1, *here))
    barrier = pltpu.get_barrier_semaphore()
    for partner in partners:
        pl.semaphore_signal(barrier, inc=1, device_id=partner, device_id_type=MESH)
    for copy in loads:
        copy.start()

    loads[0].wait()

    def take_edge(r, carry):
        edge32[0, pl.ds(r, 1), :] = cot[r, 0:16, :].astype(F32)[0:1]
        edge32[1, pl.ds(r, 1), :] = cot[r, COLS - 16 : COLS, :].astype(F32)[15:16]
        return carry

    lax.fori_loop(0, ROWS, take_edge, 0, unroll=4)
    edge[...] = edge32[...].astype(BF)

    pl.semaphore_wait(barrier, len(partners))

    def push(src, dst, send, recv, to):
        copy = pltpu.make_async_remote_copy(
            src_ref=src, dst_ref=dst, send_sem=send, recv_sem=recv,
            device_id=to, device_id_type=MESH,
        )
        copy.start()
        return copy

    sent = []
    for d in range(1, 8):
        to = (col + d) % 8
        push(
            coarse_hbm.at[pl.ds(to * 32, 32)], got_coarse.at[col],
            out_sem.at[0], in_sem.at[0], (row, to),
        )
    down, upw, right, left = (row + 1) % 16, (row + 15) % 16, (col + 1) % 8, (col + 7) % 8
    sent.append(push(edge.at[1], got_edge.at[0], out_sem.at[1], in_sem.at[1], (row, right)))
    sent.append(push(edge.at[0], got_edge.at[1], out_sem.at[2], in_sem.at[2], (row, left)))
    sent.append(push(cot_hbm.at[ROWS - 1], got_row.at[0], out_sem.at[3], in_sem.at[3], (down, col)))
    sent.append(push(cot_hbm.at[0], got_row.at[1], out_sem.at[4], in_sem.at[4], (upw, col)))
    for n, (src_row, first, to) in enumerate(
        (
            (ROWS - 1, COLS - 16, (down, right)),
            (ROWS - 1, 0, (down, left)),
            (0, COLS - 16, (upw, right)),
            (0, 0, (upw, left)),
        )
    ):
        sent.append(
            push(
                cot_hbm.at[src_row, pl.ds(first, 16)], got_corner.at[n],
                out_sem.at[5 + n], in_sem.at[5 + n], to,
            )
        )

    loads[1].wait()
    picked = ss[pl.ds(ts_ref[0], 1), :]

    def scaled(raw):
        return (raw.astype(F32) * picked).astype(BF)

    def shift_row(r, carry):
        mid = scaled(cot[r])
        wide = mid.astype(F32)
        at = pl.ds(pl.multiple_of((r + 1) * COLS, COLS), COLS)
        dcat[at, C : 2 * C] = mid
        dcat[at, 2 * C : 3 * C] = pltpu.roll(wide, 1, 0).astype(BF)
        dcat[at, 0:C] = pltpu.roll(wide, COLS - 1, 0).astype(BF)
        return carry

    lax.fori_loop(0, ROWS, shift_row, 0, unroll=2)

    loads[2].wait()
    for i in range(3):
        for j in range(3):
            wcat[i, j * C : (j + 1) * C, :] = w[3 * i + j].T

    keep_top = jnp.where(row > 0, 1.0, 0.0)
    keep_bottom = jnp.where(row < 15, 1.0, 0.0)
    keep_left = jnp.where(col > 0, 1.0, 0.0)
    keep_right = jnp.where(col < 7, 1.0, 0.0)

    for copy in sent:
        copy.wait()
    patch[0] = scaled(got_edge[0]).astype(F32) * keep_left
    patch[1] = scaled(got_edge[1]).astype(F32) * keep_right
    spot = lax.broadcasted_iota(jnp.int32, (16, C), 0)

    def patch_row(r, carry):
        first = pl.ds(pl.multiple_of((r + 1) * COLS, COLS), 16)
        last = pl.ds(pl.multiple_of((r + 1) * COLS + COLS - 16, 16), 16)
        lo = dcat[first, 2 * C : 3 * C].astype(F32)
        dcat[first, 2 * C : 3 * C] = jnp.where(spot == 0, patch[0, pl.ds(r, 1), :], lo).astype(BF)
        hi = dcat[last, 0:C].astype(F32)
        dcat[last, 0:C] = jnp.where(spot == 15, patch[1, pl.ds(r, 1), :], hi).astype(BF)
        return carry

    lax.fori_loop(0, ROWS, patch_row, 0, unroll=4)
    spot_row = lax.broadcasted_iota(jnp.int32, (COLS, C), 0)
    for n, (start, keep) in enumerate(((0, keep_top), ((ROWS + 1) * COLS, keep_bottom))):
        wide = scaled(got_row[n]).astype(F32) * keep
        near = scaled(got_corner[2 * n]).astype(F32)[15:16] * (keep * keep_left)
        far = scaled(got_corner[2 * n + 1]).astype(F32)[0:1] * (keep * keep_right)
        at = pl.ds(start, COLS)
        dcat[at, C : 2 * C] = wide.astype(BF)
        dcat[at, 2 * C : 3 * C] = jnp.where(spot_row == 0, near, pltpu.roll(wide, 1, 0)).astype(BF)
        dcat[at, 0:C] = jnp.where(
            spot_row == COLS - 1, far, pltpu.roll(wide, COLS - 1, 0)
        ).astype(BF)

    loads[3].wait()
    loads[4].wait()
    seven = got_coarse.at[pl.ds(0, 7)]
    pltpu.make_async_copy(seven, seven, in_sem.at[0]).wait()

    def activate(r, carry):
        @pl.when(r % 4 == 0)
        def _():
            coarse = got_coarse[r // 4].astype(F32)
            for n in range(4):
                for half in range(2):
                    up[half, pl.ds(n, 32, stride=4), :] = coarse[:, half * 128 : half * 128 + 128]

        hidden = fine[r].astype(F32) + jnp.concatenate([up[0], up[1]], axis=1)
        sig = 0.5 * jnp.tanh(0.5 * hidden) + 0.5
        value = hidden * sig
        at = pl.ds(pl.multiple_of(r * COLS, COLS), COLS)
        act[at, :] = value.astype(BF)
        slope[at, :] = sig + value * (1.0 - sig)
        return carry

    lax.fori_loop(0, ROWS, activate, 0)

    def order(j):
        return ((0, 1, 2), (1, 2, 0), (2, 0, 1))[j]

    def mine(j):
        return here[order(j)[0]] * 2 + k

    def group(j):
        axis = order(j)[0]
        return [
            (d, flip, ((here[axis] + d) % 4) * 2 + (k + flip) % 2, other(axis, d, flip, *here))
            for d in range(4)
            for flip in range(2)
            if d or flip
        ]

    def taps(i, carry):
        at = pl.ds(pl.multiple_of((2 - i) * COLS, COLS), PIX)
        for j in range(3):
            t = i * 3 + j
            part[t] = lax.dot_general(
                act[...], dcat[at, j * C : (j + 1) * C], TN, preferred_element_type=F32
            ).astype(BF)
            for _, _, m, to in group(j):
                push(
                    part.at[t, pl.ds(m * PIECE, PIECE)], stack1.at[t, mine(j)],
                    ar_out.at[0, t], ar_in.at[0, t], to,
                )
            stack1[t, mine(j)] = part[t, pl.ds(pl.multiple_of(mine(j) * PIECE, PIECE), PIECE), :]
        return carry

    lax.fori_loop(0, 3, taps, 0)

    def total(stack, t, count):
        out = stack[t, 0].astype(F32)
        for n in range(1, count):
            out = out + stack[t, n].astype(F32)
        return out.astype(BF)

    def arrived(stack, t, count, sem):
        some = stack.at[t, pl.ds(0, count)]
        pltpu.make_async_copy(some, some, sem).wait()

    def exchange(stack, t, j, phase):
        axis = order(j)[phase]
        for d in range(1, 4):
            push(
                stack.at[t, here[axis]], stack.at[t, here[axis]],
                ar_out.at[phase, t], ar_in.at[phase, t], other(axis, d, 0, *here),
            )

    def step1(i):
        for j in range(3):
            t = i * 3 + j
            arrived(stack1, t, 7, ar_in.at[0, t])
            stack2[t, here[order(j)[1]]] = total(stack1, t, 8)
            exchange(stack2, t, j, 1)

    def step2(i):
        for j in range(3):
            t = i * 3 + j
            arrived(stack2, t, 3, ar_in.at[1, t])
            stack3[t, here[order(j)[2]]] = total(stack2, t, 4)
            exchange(stack3, t, j, 2)

    def step3(i):
        for j in range(3):
            t = i * 3 + j
            arrived(stack3, t, 3, ar_in.at[2, t])
            at = pl.ds(pl.multiple_of(mine(j) * PIECE, PIECE), PIECE)
            whole[t, at, :] = total(stack3, t, 4)
            for _, _, _, to in group(j):
                push(whole.at[t, at], whole.at[t, at], ar_out.at[3, t], ar_in.at[3, t], to)

    scale = 1.0 / math.sqrt(PIX * GRID[0] * GRID[1])

    def step4(i):
        for j in range(3):
            t = i * 3 + j
            some = whole.at[t, pl.ds(0, 7 * PIECE)]
            pltpu.make_async_copy(some, some, ar_in.at[3, t]).wait()
            gw_ref[t] = whole[t].astype(F32) * scale

    def strip(n, carry):
        c = (col + 1 + n) % 8
        base = c * (4 * COLS)
        acc = None
        for i in range(3):
            at = pl.ds(pl.multiple_of(base + (2 - i) * COLS, COLS), 4 * COLS)
            term = jnp.dot(dcat[at, :], wcat[i], preferred_element_type=F32)
            acc = term if acc is None else acc + term
        at = pl.ds(pl.multiple_of(base, COLS), 4 * COLS)
        dh = acc * slope[at, :]
        gf_ref[at, :] = dh.astype(BF)
        tall = dh[0:COLS] + dh[COLS : 2 * COLS] + dh[2 * COLS : 3 * COLS] + dh[3 * COLS :]
        for half in range(2):
            lanes = slice(half * 128, half * 128 + 128)
            pooled_rows[half] = tall[:, lanes]
            cells = pooled_rows[half, pl.ds(0, 32, stride=4), :]
            for q in range(1, 4):
                cells = cells + pooled_rows[half, pl.ds(q, 32, stride=4), :]
            pool[n, :, lanes] = cells.astype(BF)
        slot = pl.ds(pl.multiple_of(col * 32, 32), 32)

        @pl.when(n < 7)
        def _():
            push(pool.at[n], got_pool.at[slot], pool_out, pool_in, (row, c))

        @pl.when(n == 7)
        def _():
            got_pool[slot, :] = pool[n]

        return carry

    plan = (
        (1, [(step1, 0)]),
        (3, [(step1, 1)]),
        (5, [(step2, 0), (step1, 2)]),
        (7, [(step2, 1)]),
        (8, [(step3, 0), (step2, 2), (step3, 1), (step3, 2)]),
    )
    done = 0
    for until, steps in plan:
        lax.fori_loop(done, until, strip, 0)
        done = until
        for step, i in steps:
            step(i)

    some = got_pool.at[pl.ds(0, 7 * 32)]
    pltpu.make_async_copy(some, some, pool_in).wait()
    gc_ref[...] = got_pool[...]
    for i in range(3):
        step4(i)

    seven = pool.at[pl.ds(0, 7)]
    pltpu.make_async_copy(seven, seven, pool_out).wait()
    seven = got_coarse.at[pl.ds(0, 7)]
    pltpu.make_async_copy(seven, seven, out_sem.at[0]).wait()
    for t in range(9):
        for phase, count in ((0, 7), (1, 3), (2, 3), (3, 7)):
            some = stack1.at[t, pl.ds(0, count)]
            pltpu.make_async_copy(some, some, ar_out.at[phase, t]).wait()


def store_kernel(gf_ref, gc_ref, gw_ref, gf_out, gc_out, gw_out, sem):
    copies = [
        pltpu.make_async_copy(src, dst, sem.at[n])
        for n, (src, dst) in enumerate(((gw_ref, gw_out), (gf_ref, gf_out), (gc_ref, gc_out)))
    ]
    for copy in copies:
        copy.start()
    for copy in copies:
        copy.wait()


def per_device(fine_input, coarse_feat, conv_weight, step_scale, timesteps, cotangent):
    anywhere = pl.BlockSpec(memory_space=pl.ANY)
    vmem = pl.BlockSpec(memory_space=pltpu.VMEM)
    buf = pltpu.VMEM
    dma = pltpu.SemaphoreType.DMA
    results = pl.pallas_call(
        fused_kernel,
        name="fused",
        out_shape=(
            pltpu.VMEM((PIX, C), BF),
            pltpu.VMEM((C, C), BF),
            pltpu.VMEM((9, C, C), F32),
        ),
        in_specs=[pl.BlockSpec(memory_space=pltpu.SMEM)] + [anywhere] * 5,
        out_specs=(vmem, vmem, vmem),
        scratch_shapes=[
            buf((1000, C), F32),
            buf((ROWS, COLS, C), BF),
            buf((ROWS, COLS, C), BF),
            buf((9, C, C), BF),
            buf((3, 3 * C, C), BF),
            buf(((ROWS + 2) * COLS, 3 * C), BF),
            buf((PIX, C), BF),
            buf((PIX, C), F32),
            buf((2, ROWS, C), F32),
            buf((2, ROWS, C), BF),
            buf((2, ROWS, C), BF),
            buf((2, COLS, C), BF),
            buf((4, 16, C), BF),
            buf((8, 32, C), BF),
            buf((2, COLS, 128), F32),
            buf((2, ROWS, C), F32),
            buf((8, 32, C), BF),
            buf((C, C), BF),
            buf((9, C, C), BF),
            buf((9, 8, PIECE, C), BF),
            buf((9, 4, PIECE, C), BF),
            buf((9, 4, PIECE, C), BF),
            buf((9, C, C), BF),
            buf((2, COLS, 128), F32),
            dma((5,)),
            dma((9,)),
            dma((9,)),
            dma,
            dma,
            dma((4, 9)),
            dma((4, 9)),
        ],
        compiler_params=pltpu.CompilerParams(
            collective_id=0, has_side_effects=True, vmem_limit_bytes=48 * 2**20
        ),
        cost_estimate=pl.CostEstimate(
            flops=2 * 2 * 9 * PIX * C * C, bytes_accessed=12 * 2**20, transcendentals=PIX * C
        ),
    )(
        timesteps,
        step_scale,
        fine_input.reshape(ROWS, COLS, C),
        coarse_feat.reshape(C, C),
        conv_weight.reshape(9, C, C),
        cotangent.reshape(ROWS, COLS, C),
    )
    gf, gc, gw = pl.pallas_call(
        store_kernel,
        name="store",
        out_shape=(
            jax.ShapeDtypeStruct((PIX, C), BF),
            jax.ShapeDtypeStruct((C, C), BF),
            jax.ShapeDtypeStruct((9, C, C), F32),
        ),
        in_specs=[vmem] * 3,
        out_specs=(anywhere, anywhere, anywhere),
        scratch_shapes=[dma((3,))],
    )(*results)
    return gf.reshape(1, ROWS, COLS, C), gc.reshape(1, 1, C, C), gw.reshape(3, 3, C, C)


def solution(mesh):
    return jax.shard_map(
        per_device,
        mesh=mesh,
        in_specs=(
            P(None, "row", "col", None),
            P(None, ("row", "col"), None, None),
            P(),
            P(),
            P(),
            P(None, "row", "col", None),
        ),
        out_specs=(P(None, "row", "col", None), P(None, ("row", "col"), None, None), P()),
        check_vma=False,
    )
```

```python
import functools
import math

import jax
import jax.numpy as jnp
from jax import lax
from jax.experimental import pallas as pl
from jax.experimental.pallas import tpu as pltpu
from jax.sharding import PartitionSpec as P

MESH = pl.DeviceIdType.MESH
BF = jnp.bfloat16
F32 = jnp.float32
ROWS, COLS, C = 32, 128, 256
PIX = ROWS * COLS
GRID = (16, 8)
STRIPS = 8
PIECE = C // 8
HALF = C // 2
WHEN = ((1, 2, 3), (4, 6, 7), (8, 10, 11), (12, 13, 14), (15, 16, 17), (16, 17, 18))


def place(x, y, z, k):
    return (y * 4 + (z // 2) * 2 + k, (z % 2) * 4 + x)


def other(axis, d, flip, x, y, z, k):
    at = [x, y, z]
    at[axis] = (at[axis] + d) % 4
    return place(*at, (k + flip) % 2)


def fused_kernel(
    ts_ref, ss_hbm, fine_hbm, coarse_hbm, w_hbm, cot_hbm,
    gf_ref, gc_ref, gw_ref,
    ss, cot, fine, w, wcat, dcat, act_t, slope,
    edge32, edge, got_edge, got_row, got_corner, got_coarse, up, patch,
    pool, got_pool, part, pair, half_sum, stack1, stack2, stack3, whole, pooled_rows,
    load_sem, out_sem, in_sem, coarse_out, coarse_in, pool_out, pool_in, ar_out, ar_in,
):
    row, col = lax.axis_index("row"), lax.axis_index("col")
    y, z_hi, k, z_lo, x = row // 4, (row // 2) % 2, row % 2, col // 4, col % 4
    z = z_hi * 2 + z_lo
    here = (x, y, z, k)
    twin = place(x, y, z, 1 - k)

    down, upw, right, left = (row + 1) % 16, (row + 15) % 16, (col + 1) % 8, (col + 7) % 8
    partners = [(row, (col + d) % 8) for d in range(1, 8)]
    partners += [(down, col), (upw, col)]
    partners += [(a, b) for a in (down, upw) for b in (left, right)]
    partners += [other(1, d, 0, *here) for d in range(1, 4)]
    partners += [place(x, y, (z + 2) % 4, k), place(x, y, 3 - z, k)]
    barrier = pltpu.get_barrier_semaphore()
    for partner in partners:
        pl.semaphore_signal(barrier, inc=1, device_id=partner, device_id_type=MESH)

    loads = [
        pltpu.make_async_copy(cot_hbm, cot, load_sem.at[0]),
        pltpu.make_async_copy(ss_hbm, ss, load_sem.at[1]),
        pltpu.make_async_copy(w_hbm, w, load_sem.at[2]),
        pltpu.make_async_copy(fine_hbm, fine, load_sem.at[3]),
        pltpu.make_async_copy(
            coarse_hbm.at[pl.ds(col * 32, 32)], got_coarse.at[col], load_sem.at[4]
        ),
    ]
    for copy in loads:
        copy.start()

    loads[0].wait()

    def take_edge(r, carry):
        edge32[0, pl.ds(r, 1), :] = cot[r, 0:16, :].astype(F32)[0:1]
        edge32[1, pl.ds(r, 1), :] = cot[r, COLS - 16 : COLS, :].astype(F32)[15:16]
        return carry

    lax.fori_loop(0, ROWS, take_edge, 0, unroll=8)
    edge[...] = edge32[...].astype(BF)

    pl.semaphore_wait(barrier, len(partners))

    def push(src, dst, send, recv, to):
        copy = pltpu.make_async_remote_copy(
            src_ref=src, dst_ref=dst, send_sem=send, recv_sem=recv,
            device_id=to, device_id_type=MESH,
        )
        copy.start()
        return copy

    def near_strip(n):
        m = n % 4
        return ((z_lo + n // 4) % 2) * 4 + (x + (m * (m + 1) // 2)) % 4

    for n in range(7, 0, -1):
        to = near_strip(n)
        push(
            coarse_hbm.at[pl.ds(to * 32, 32)], got_coarse.at[col],
            coarse_out, coarse_in.at[col], (row, to),
        )
    sent = []
    for n, (src_row, first, to) in enumerate(
        (
            (ROWS - 1, COLS - 16, (down, right)),
            (ROWS - 1, 0, (down, left)),
            (0, COLS - 16, (upw, right)),
            (0, 0, (upw, left)),
        )
    ):
        sent.append(
            push(
                cot_hbm.at[src_row, pl.ds(first, 16)], got_corner.at[n],
                out_sem.at[n], in_sem.at[n], to,
            )
        )
    sent.append(push(cot_hbm.at[ROWS - 1], got_row.at[0], out_sem.at[4], in_sem.at[4], (down, col)))
    sent.append(push(cot_hbm.at[0], got_row.at[1], out_sem.at[5], in_sem.at[5], (upw, col)))
    sent.append(push(edge.at[1], got_edge.at[0], out_sem.at[6], in_sem.at[6], (row, right)))
    sent.append(push(edge.at[0], got_edge.at[1], out_sem.at[7], in_sem.at[7], (row, left)))

    loads[1].wait()
    picked = ss[pl.ds(ts_ref[0], 1), :]

    def scaled(raw):
        return (raw.astype(F32) * picked).astype(BF)

    def shift_row(r, carry):
        mid = scaled(cot[r])
        wide = mid.astype(F32)
        at = pl.ds(pl.multiple_of((r + 1) * COLS, COLS), COLS)
        dcat[at, C : 2 * C] = mid
        dcat[at, 2 * C : 3 * C] = pltpu.roll(wide, 1, 0).astype(BF)
        dcat[at, 0:C] = pltpu.roll(wide, COLS - 1, 0).astype(BF)
        return carry

    lax.fori_loop(0, ROWS, shift_row, 0, unroll=2)

    loads[2].wait()

    def turn_weight(i, carry):
        for j in range(3):
            wcat[i, j * C : (j + 1) * C, :] = w[3 * i + j].T
        return carry

    lax.fori_loop(0, 3, turn_weight, 0)

    loads[3].wait()
    loads[4].wait()

    def activate(n, carry):
        strip = near_strip(n)

        @pl.when(n > 0)
        def _():
            some = got_coarse.at[strip]
            pltpu.make_async_copy(some, some, coarse_in.at[strip]).wait()

        coarse = got_coarse[strip].astype(F32)
        for q in range(4):
            for half in range(2):
                up[half, pl.ds(q, 32, stride=4), :] = coarse[:, half * 128 : half * 128 + 128]

        def fine_row(q, carry):
            r = strip * 4 + q
            hidden = fine[r].astype(F32) + jnp.concatenate([up[0], up[1]], axis=1)
            sig = 0.5 * jnp.tanh(0.5 * hidden) + 0.5
            value = hidden * sig
            at = pl.ds(pl.multiple_of(r * COLS, COLS), COLS)
            act_t[:, at] = value.astype(BF).T
            slope[at, :] = sig + value * (1.0 - sig)
            return carry

        return lax.fori_loop(0, 4, fine_row, carry, unroll=2)

    lax.fori_loop(0, STRIPS, activate, 0)

    keep_top = jnp.where(row > 0, 1.0, 0.0)
    keep_bottom = jnp.where(row < 15, 1.0, 0.0)
    keep_left = jnp.where(col > 0, 1.0, 0.0)
    keep_right = jnp.where(col < 7, 1.0, 0.0)

    for copy in sent:
        copy.wait()
    patch[0] = scaled(got_edge[0]).astype(F32) * keep_left
    patch[1] = scaled(got_edge[1]).astype(F32) * keep_right
    spot = lax.broadcasted_iota(jnp.int32, (16, C), 0)

    def patch_row(r, carry):
        first = pl.ds(pl.multiple_of((r + 1) * COLS, COLS), 16)
        last = pl.ds(pl.multiple_of((r + 1) * COLS + COLS - 16, 16), 16)
        lo = dcat[first, 2 * C : 3 * C].astype(F32)
        dcat[first, 2 * C : 3 * C] = jnp.where(spot == 0, patch[0, pl.ds(r, 1), :], lo).astype(BF)
        hi = dcat[last, 0:C].astype(F32)
        dcat[last, 0:C] = jnp.where(spot == 15, patch[1, pl.ds(r, 1), :], hi).astype(BF)
        return carry

    lax.fori_loop(0, ROWS, patch_row, 0, unroll=4)
    spot_row = lax.broadcasted_iota(jnp.int32, (COLS, C), 0)
    for n, (start, keep) in enumerate(((0, keep_top), ((ROWS + 1) * COLS, keep_bottom))):
        wide = scaled(got_row[n]).astype(F32) * keep
        near = scaled(got_corner[2 * n]).astype(F32)[15:16] * (keep * keep_left)
        far = scaled(got_corner[2 * n + 1]).astype(F32)[0:1] * (keep * keep_right)
        at = pl.ds(start, COLS)
        dcat[at, C : 2 * C] = wide.astype(BF)
        dcat[at, 2 * C : 3 * C] = jnp.where(spot_row == 0, near, pltpu.roll(wide, 1, 0)).astype(BF)
        dcat[at, 0:C] = jnp.where(
            spot_row == COLS - 1, far, pltpu.roll(wide, COLS - 1, 0)
        ).astype(BF)

    my_half = pl.ds(pl.multiple_of(k * HALF, HALF), HALF)
    twin_half = pl.ds(pl.multiple_of((1 - k) * HALF, HALF), HALF)

    def one_hot(axis):
        return (1 - axis) * (2 - axis) // 2, axis * (2 - axis), axis * (axis - 1) // 2

    def mine(axis):
        a, b, c = one_hot(axis)
        return a * x + b * y + c * z

    def peers(axis):
        a, b, c = one_hot(axis)
        me = mine(axis)
        for d in range(1, 4):
            yield (me + d) % 4, place((x + d * a) % 4, (y + d * b) % 4, (z + d * c) % 4, k)

    def arrived(some, sem):
        pltpu.make_async_copy(some, some, sem).wait()

    def total(stack, t):
        out = stack[t, 0].astype(F32)
        for n in range(1, 4):
            out = out + stack[t, n].astype(F32)
        return out.astype(BF)

    def quarter(m):
        return pl.ds(pl.multiple_of(m * PIECE, PIECE), PIECE)

    def step0(t, j):
        arrived(pair.at[t], ar_in.at[0, t])
        half_sum[t] = (part[t, my_half, :].astype(F32) + pair[t].astype(F32)).astype(BF)
        me = mine(j)
        for m, to in peers(j):
            push(half_sum.at[t, quarter(m)], stack1.at[t, me], ar_out.at[1, t], ar_in.at[1, t], to)
        stack1[t, me] = half_sum[t, quarter(me), :]

    def exchange(before, after, phase):
        def step(t, j):
            arrived(before.at[t, pl.ds(0, 3)], ar_in.at[phase, t])
            axis = (j + phase) % 3
            me = mine(axis)
            after[t, me] = total(before, t)
            for _, to in peers(axis):
                push(
                    after.at[t, me], after.at[t, me],
                    ar_out.at[phase + 1, t], ar_in.at[phase + 1, t], to,
                )

        return step

    def step3(t, j):
        arrived(stack3.at[t, pl.ds(0, 3)], ar_in.at[3, t])
        at = quarter(4 * k + mine(j))
        whole[t, at, :] = total(stack3, t)
        for _, to in peers(j):
            push(whole.at[t, at], whole.at[t, at], ar_out.at[4, t], ar_in.at[4, t], to)

    def step4(t, j):
        arrived(whole.at[t, pl.ds(0, 3 * PIECE)], ar_in.at[4, t])
        push(whole.at[t, my_half], whole.at[t, my_half], ar_out.at[5, t], ar_in.at[5, t], twin)

    scale = 1.0 / math.sqrt(PIX * GRID[0] * GRID[1])

    def step5(t, j):
        arrived(whole.at[t, pl.ds(0, HALF)], ar_in.at[5, t])
        gw_ref[t] = whole[t].astype(F32) * scale

    def first_tap(g):
        return 3 * ((4 - g) % 3)

    def taps(g):
        first = first_tap(g)
        at = pl.ds(pl.multiple_of(2 * COLS - first // 3 * COLS, COLS), PIX)
        for j in range(3):
            part[first + j] = jnp.dot(
                act_t[...], dcat[at, j * C : (j + 1) * C], preferred_element_type=F32
            ).astype(BF)
        for j in range(3):
            t = first + j
            push(part.at[t, twin_half], pair.at[t], ar_out.at[0, t], ar_in.at[0, t], twin)

    def strip(n):
        c = (col + 1 + n) % 8
        base = c * (4 * COLS)
        acc = None
        for i in range(3):
            at = pl.ds(pl.multiple_of(base + (2 - i) * COLS, COLS), 4 * COLS)
            term = jnp.dot(dcat[at, :], wcat[i], preferred_element_type=F32)
            acc = term if acc is None else acc + term
        at = pl.ds(pl.multiple_of(base, COLS), 4 * COLS)
        dh = acc * slope[at, :]
        gf_ref[at, :] = dh.astype(BF)
        tall = dh[0:COLS] + dh[COLS : 2 * COLS] + dh[2 * COLS : 3 * COLS] + dh[3 * COLS :]
        for half in range(2):
            lanes = slice(half * 128, half * 128 + 128)
            pooled_rows[half] = tall[:, lanes]
            cells = pooled_rows[half, pl.ds(0, 32, stride=4), :]
            for q in range(1, 4):
                cells = cells + pooled_rows[half, pl.ds(q, 32, stride=4), :]
            pool[n, :, lanes] = cells.astype(BF)
        slot = pl.ds(pl.multiple_of(col * 32, 32), 32)

        @pl.when(n < 7)
        def _():
            push(pool.at[n], got_pool.at[slot], pool_out, pool_in, (row, c))

        @pl.when(n == 7)
        def _():
            got_pool[slot, :] = pool[n]

    steps = (step0, exchange(stack1, stack2, 1), exchange(stack2, stack3, 2), step3, step4, step5)

    def slot(u, carry):
        @pl.when(u < 3)
        def _():
            taps(u)

        @pl.when((u >= 3) & (u < 3 + STRIPS))
        def _():
            strip(u - 3)

        for step, (first, second, third) in zip(steps, WHEN):
            @pl.when((u == first) | (u == second) | (u == third))
            def _():
                g = jnp.where(u == first, 0, jnp.where(u == second, 1, 2))
                lax.fori_loop(0, 3, lambda j, c: (step(first_tap(g) + j, j), c)[1], 0)

        return carry

    lax.fori_loop(0, WHEN[-1][-1] + 1, slot, 0)

    arrived(got_pool.at[pl.ds(0, 7 * 32)], pool_in)
    gc_ref[...] = got_pool[...]

    arrived(pool.at[pl.ds(0, 7)], pool_out)
    arrived(got_coarse.at[pl.ds(0, 7)], coarse_out)

    def left(t, carry):
        for phase in range(6):
            rows = HALF if phase in (0, 5) else 3 * PIECE
            arrived(part.at[t, pl.ds(0, rows)], ar_out.at[phase, t])
        return carry

    lax.fori_loop(0, 9, left, 0)


def store_kernel(gf_ref, gc_ref, gw_ref, gf_out, gc_out, gw_out, sem):
    pairs = [(gw_ref.at[t], gw_out.at[t]) for t in range(9)]
    for n in range(8):
        some = pl.ds(n * (PIX // 8), PIX // 8)
        pairs.append((gf_ref.at[some], gf_out.at[some]))
    pairs.append((gc_ref, gc_out))
    copies = [pltpu.make_async_copy(*pair, sem.at[n]) for n, pair in enumerate(pairs)]
    for copy in copies:
        copy.start()
    for copy in copies:
        copy.wait()


def per_device(fine_input, coarse_feat, conv_weight, step_scale, timesteps, cotangent):
    anywhere = pl.BlockSpec(memory_space=pl.ANY)
    vmem = pl.BlockSpec(memory_space=pltpu.VMEM)
    buf = pltpu.VMEM
    dma = pltpu.SemaphoreType.DMA
    def in_hbm(array, shape):
        return pltpu.with_memory_space_constraint(array.reshape(shape), pltpu.HBM)

    results = pl.pallas_call(
        fused_kernel,
        name="fused",
        out_shape=(
            pltpu.VMEM((PIX, C), BF),
            pltpu.VMEM((C, C), BF),
            pltpu.VMEM((9, C, C), F32),
        ),
        in_specs=[pl.BlockSpec(memory_space=pltpu.SMEM)] + [anywhere] * 5,
        out_specs=(vmem, vmem, vmem),
        scratch_shapes=[
            buf((1000, C), F32),
            buf((ROWS, COLS, C), BF),
            buf((ROWS, COLS, C), BF),
            buf((9, C, C), BF),
            buf((3, 3 * C, C), BF),
            buf(((ROWS + 2) * COLS, 3 * C), BF),
            buf((C, PIX), BF),
            buf((PIX, C), F32),
            buf((2, ROWS, C), F32),
            buf((2, ROWS, C), BF),
            buf((2, ROWS, C), BF),
            buf((2, COLS, C), BF),
            buf((4, 16, C), BF),
            buf((8, 32, C), BF),
            buf((2, COLS, 128), F32),
            buf((2, ROWS, C), F32),
            buf((8, 32, C), BF),
            buf((C, C), BF),
            buf((9, C, C), BF),
            buf((9, HALF, C), BF),
            buf((9, HALF, C), BF),
            buf((9, 4, PIECE, C), BF),
            buf((9, 4, PIECE, C), BF),
            buf((9, 4, PIECE, C), BF),
            buf((9, C, C), BF),
            buf((2, COLS, 128), F32),
            dma((5,)),
            dma((8,)),
            dma((8,)),
            dma,
            dma((8,)),
            dma,
            dma,
            dma((6, 9)),
            dma((6, 9)),
        ],
        compiler_params=pltpu.CompilerParams(
            collective_id=0, has_side_effects=True, vmem_limit_bytes=40 * 2**20
        ),
        cost_estimate=pl.CostEstimate(
            flops=2 * 2 * 9 * PIX * C * C, bytes_accessed=12 * 2**20, transcendentals=PIX * C
        ),
    )(
        timesteps,
        in_hbm(step_scale, step_scale.shape),
        in_hbm(fine_input, (ROWS, COLS, C)),
        in_hbm(coarse_feat, (C, C)),
        in_hbm(conv_weight, (9, C, C)),
        in_hbm(cotangent, (ROWS, COLS, C)),
    )
    gf, gc, gw = pl.pallas_call(
        store_kernel,
        name="store",
        out_shape=(
            jax.ShapeDtypeStruct((PIX, C), BF),
            jax.ShapeDtypeStruct((C, C), BF),
            jax.ShapeDtypeStruct((9, C, C), F32),
        ),
        in_specs=[vmem] * 3,
        out_specs=(anywhere, anywhere, anywhere),
        scratch_shapes=[dma((18,))],
        compiler_params=pltpu.CompilerParams(vmem_limit_bytes=2**20),
    )(*(pltpu.with_memory_space_constraint(result, pltpu.VMEM) for result in results))
    return gf.reshape(1, ROWS, COLS, C), gc.reshape(1, 1, C, C), gw.reshape(3, 3, C, C)


def solution(mesh):
    return jax.shard_map(
        per_device,
        mesh=mesh,
        in_specs=(
            P(None, "row", "col", None),
            P(None, ("row", "col"), None, None),
            P(),
            P(),
            P(),
            P(None, "row", "col", None),
        ),
        out_specs=(P(None, "row", "col", None), P(None, ("row", "col"), None, None), P()),
        check_vma=False,
    )
```

```python
import functools
import math

import jax
import jax.numpy as jnp
from jax import lax
from jax.experimental import pallas as pl
from jax.experimental.pallas import tpu as pltpu
from jax.sharding import PartitionSpec as P

MESH = pl.DeviceIdType.MESH
BF = jnp.bfloat16
F32 = jnp.float32
ROWS, COLS, C = 32, 128, 256
PIX = ROWS * COLS
GRID = (16, 8)
STRIPS = 8
PIECE = C // 8
WHEN = ((2, 5, 7), (7, 10, 11), (11, 12, 13), (14, 15, 16))


def place(x, y, z, k):
    return (y * 4 + (z // 2) * 2 + k, (z % 2) * 4 + x)


def other(axis, d, flip, x, y, z, k):
    at = [x, y, z]
    at[axis] = (at[axis] + d) % 4
    return place(*at, (k + flip) % 2)


def fused_kernel(
    ts, ss_hbm, fine_hbm, coarse_hbm, w_hbm, cot_hbm,
    gf_ref, gc_ref, gw_ref,
    ss, cot, fine, coarse, w, wcat, dcat, act_t, slope,
    edge32, edge, got_edge, got_row, got_corner, got_coarse, up, patch,
    pool, got_pool, part, stack1, stack2, stack3, whole, pooled_rows,
    load_sem, out_sem, in_sem, coarse_out, coarse_in, pool_out, pool_in, ar_out, ar_in,
):
    row, col = lax.axis_index("row"), lax.axis_index("col")
    y, z_hi, k, z_lo, x = row // 4, (row // 2) % 2, row % 2, col // 4, col % 4
    z = z_hi * 2 + z_lo
    here = (x, y, z, k)

    down, upw, right, left = (row + 1) % 16, (row + 15) % 16, (col + 1) % 8, (col + 7) % 8
    partners = [(row, (col + d) % 8) for d in range(1, 8)]
    partners += [(down, col), (upw, col)]
    partners += [(a, b) for a in (down, upw) for b in (left, right)]
    partners += [other(1, d, 0, *here) for d in range(1, 4)]
    partners += [place(x, y, (z + 2) % 4, k), place(x, y, 3 - z, k)]
    partners += [other(axis, d, 1, *here) for axis in range(3) for d in range(1, 4)]
    barrier = pltpu.get_barrier_semaphore()
    for partner in partners:
        pl.semaphore_signal(barrier, inc=1, device_id=partner, device_id_type=MESH)

    loads = [
        pltpu.make_async_copy(src, dst, load_sem.at[n])
        for n, (src, dst) in enumerate(
            (
                (coarse_hbm, coarse), (cot_hbm, cot),
                (ss_hbm, ss), (w_hbm, w), (fine_hbm, fine),
            )
        )
    ]
    for copy in loads:
        copy.start()

    def push(src, dst, send, recv, to):
        copy = pltpu.make_async_remote_copy(
            src_ref=src, dst_ref=dst, send_sem=send, recv_sem=recv,
            device_id=to, device_id_type=MESH,
        )
        copy.start()
        return copy

    def near_strip(n):
        m = n % 4
        return ((z_lo + n // 4) % 2) * 4 + (x + (m * (m + 1) // 2)) % 4

    loads[0].wait()
    pl.semaphore_wait(barrier, len(partners))
    for n in range(7, 0, -1):
        to = near_strip(n)
        push(
            coarse.at[pl.ds(pl.multiple_of(to * 32, 32), 32)], got_coarse.at[col],
            coarse_out, coarse_in.at[col], (row, to),
        )

    loads[1].wait()

    def take_edge(r, carry):
        edge32[0, pl.ds(r, 1), :] = cot[r, 0:16, :].astype(F32)[0:1]
        edge32[1, pl.ds(r, 1), :] = cot[r, COLS - 16 : COLS, :].astype(F32)[15:16]
        return carry

    lax.fori_loop(0, ROWS, take_edge, 0, unroll=8)
    edge[...] = edge32[...].astype(BF)
    sent = [
        push(edge.at[1], got_edge.at[0], out_sem.at[0], in_sem.at[0], (row, right)),
        push(edge.at[0], got_edge.at[1], out_sem.at[1], in_sem.at[1], (row, left)),
    ]
    sent.append(push(cot.at[ROWS - 1], got_row.at[0], out_sem.at[2], in_sem.at[2], (down, col)))
    sent.append(push(cot.at[0], got_row.at[1], out_sem.at[3], in_sem.at[3], (upw, col)))
    for n, (src_row, first, to) in enumerate(
        (
            (ROWS - 1, COLS - 16, (down, right)),
            (ROWS - 1, 0, (down, left)),
            (0, COLS - 16, (upw, right)),
            (0, 0, (upw, left)),
        )
    ):
        sent.append(
            push(
                cot.at[src_row, pl.ds(first, 16)], got_corner.at[n],
                out_sem.at[4 + n], in_sem.at[4 + n], to,
            )
        )

    loads[2].wait()
    picked = ss[pl.ds(ts[0], 1), :]

    def scaled(raw):
        return (raw.astype(F32) * picked).astype(BF)

    def shift_row(r, carry):
        mid = scaled(cot[r])
        wide = mid.astype(F32)
        at = pl.ds(pl.multiple_of((r + 1) * COLS, COLS), COLS)
        dcat[at, C : 2 * C] = mid
        dcat[at, 2 * C : 3 * C] = pltpu.roll(wide, 1, 0).astype(BF)
        dcat[at, 0:C] = pltpu.roll(wide, COLS - 1, 0).astype(BF)
        return carry

    lax.fori_loop(0, ROWS, shift_row, 0, unroll=2)

    loads[3].wait()

    def turn_weight(i, carry):
        for j in range(3):
            wcat[i, j * C : (j + 1) * C, :] = w[3 * i + j].T
        return carry

    lax.fori_loop(0, 3, turn_weight, 0)

    loads[4].wait()

    def activate(n, carry):
        strip = near_strip(n)

        @pl.when(n == 0)
        def _():
            got_coarse[strip] = coarse[pl.ds(pl.multiple_of(strip * 32, 32), 32), :]

        @pl.when(n > 0)
        def _():
            some = got_coarse.at[strip]
            pltpu.make_async_copy(some, some, coarse_in.at[strip]).wait()

        cells = got_coarse[strip].astype(F32)
        for q in range(4):
            for half in range(2):
                up[half, pl.ds(q, 32, stride=4), :] = cells[:, half * 128 : half * 128 + 128]

        def fine_row(q, carry):
            r = strip * 4 + q
            hidden = fine[r].astype(F32) + jnp.concatenate([up[0], up[1]], axis=1)
            sig = 0.5 * jnp.tanh(0.5 * hidden) + 0.5
            value = hidden * sig
            at = pl.ds(pl.multiple_of(r * COLS, COLS), COLS)
            act_t[:, at] = value.astype(BF).T
            slope[at, :] = sig + value * (1.0 - sig)
            return carry

        return lax.fori_loop(0, 4, fine_row, carry, unroll=2)

    lax.fori_loop(0, STRIPS, activate, 0)

    keep_top = jnp.where(row > 0, 1.0, 0.0)
    keep_bottom = jnp.where(row < 15, 1.0, 0.0)
    keep_left = jnp.where(col > 0, 1.0, 0.0)
    keep_right = jnp.where(col < 7, 1.0, 0.0)

    for copy in sent[:2]:
        copy.wait()
    patch[0] = scaled(got_edge[0]).astype(F32) * keep_left
    patch[1] = scaled(got_edge[1]).astype(F32) * keep_right
    spot = lax.broadcasted_iota(jnp.int32, (16, C), 0)

    def patch_row(r, carry):
        first = pl.ds(pl.multiple_of((r + 1) * COLS, COLS), 16)
        last = pl.ds(pl.multiple_of((r + 1) * COLS + COLS - 16, 16), 16)
        lo = dcat[first, 2 * C : 3 * C].astype(F32)
        dcat[first, 2 * C : 3 * C] = jnp.where(spot == 0, patch[0, pl.ds(r, 1), :], lo).astype(BF)
        hi = dcat[last, 0:C].astype(F32)
        dcat[last, 0:C] = jnp.where(spot == 15, patch[1, pl.ds(r, 1), :], hi).astype(BF)
        return carry

    lax.fori_loop(0, ROWS, patch_row, 0, unroll=4)
    spot_row = lax.broadcasted_iota(jnp.int32, (COLS, C), 0)

    def outer_rows():
        for copy in sent[2:]:
            copy.wait()
        for n, (start, keep) in enumerate(((0, keep_top), ((ROWS + 1) * COLS, keep_bottom))):
            wide = scaled(got_row[n]).astype(F32) * keep
            near = scaled(got_corner[2 * n]).astype(F32)[15:16] * (keep * keep_left)
            far = scaled(got_corner[2 * n + 1]).astype(F32)[0:1] * (keep * keep_right)
            at = pl.ds(start, COLS)
            dcat[at, C : 2 * C] = wide.astype(BF)
            dcat[at, 2 * C : 3 * C] = jnp.where(
                spot_row == 0, near, pltpu.roll(wide, 1, 0)
            ).astype(BF)
            dcat[at, 0:C] = jnp.where(
                spot_row == COLS - 1, far, pltpu.roll(wide, COLS - 1, 0)
            ).astype(BF)

    def mine(axis):
        return here[axis] * 2 + k

    def eight(axis):
        return [
            (((here[axis] + d) % 4) * 2 + (k + flip) % 2, other(axis, d, flip, *here))
            for d, flip in ((2, 1), (2, 0), (1, 1), (3, 1), (1, 0), (3, 0), (0, 1))
        ]

    def peers(axis):
        return [other(axis, d, 0, *here) for d in (2, 1, 3)]

    def arrived(some, sem):
        pltpu.make_async_copy(some, some, sem).wait()

    def total(stack, t):
        out = stack[t, 0].astype(F32)
        for n in range(1, stack.shape[1]):
            out = out + stack[t, n].astype(F32)
        return out.astype(BF)

    def quarter(m):
        return pl.ds(pl.multiple_of(m * PIECE, PIECE), PIECE)

    def three(stack, first, rows):
        return stack.at[pl.ds(first, 3), pl.ds(0, rows)]

    def exchange(before, after, phase):
        def step(g, first):
            arrived(three(before, first, before.shape[1] - 1), ar_in.at[phase - 1, g])
            for j in range(3):
                after[first + j, here[(j + phase) % 3]] = total(before, first + j)
            for j in range(3):
                t, axis = first + j, (j + phase) % 3
                for to in peers(axis):
                    push(
                        after.at[t, here[axis]], after.at[t, here[axis]],
                        ar_out.at[phase], ar_in.at[phase, g], to,
                    )

        return step

    def step3(g, first):
        arrived(three(stack3, first, 3), ar_in.at[2, g])
        for j in range(3):
            whole[first + j, quarter(mine(j)), :] = total(stack3, first + j)
        for j in range(3):
            some = whole.at[first + j, quarter(mine(j))]
            for _, to in eight(j):
                push(some, some, ar_out.at[3], ar_in.at[3, g], to)

    scale = 1.0 / math.sqrt(PIX * GRID[0] * GRID[1])

    def step4(g, first):
        arrived(three(whole, first, 7 * PIECE), ar_in.at[3, g])
        for j in range(3):
            gw_ref[first + j] = whole[first + j].astype(F32) * scale

    def first_tap(g):
        return 3 * ((4 - g) % 3)

    def taps(g):
        first = first_tap(g)
        at = pl.ds(pl.multiple_of(2 * COLS - first // 3 * COLS, COLS), PIX)
        for j in range(3):
            part[first + j] = jnp.dot(
                act_t[...], dcat[at, j * C : (j + 1) * C], preferred_element_type=F32
            ).astype(BF)
        for j in range(3):
            t = first + j
            for m, to in eight(j):
                push(part.at[t, quarter(m)], stack1.at[t, mine(j)], ar_out.at[0], ar_in.at[0, g], to)
            stack1[t, mine(j)] = part[t, quarter(mine(j)), :]

    def strip(n):
        c = (col + 1 + n) % 8
        base = c * (4 * COLS)
        acc = None
        for i in range(3):
            at = pl.ds(pl.multiple_of(base + (2 - i) * COLS, COLS), 4 * COLS)
            term = jnp.dot(dcat[at, :], wcat[i], preferred_element_type=F32)
            acc = term if acc is None else acc + term
        at = pl.ds(pl.multiple_of(base, COLS), 4 * COLS)
        dh = acc * slope[at, :]
        gf_ref[at, :] = dh.astype(BF)
        tall = dh[0:COLS] + dh[COLS : 2 * COLS] + dh[2 * COLS : 3 * COLS] + dh[3 * COLS :]
        for half in range(2):
            lanes = slice(half * 128, half * 128 + 128)
            pooled_rows[half] = tall[:, lanes]
            cells = pooled_rows[half, pl.ds(0, 32, stride=4), :]
            for q in range(1, 4):
                cells = cells + pooled_rows[half, pl.ds(q, 32, stride=4), :]
            pool[n, :, lanes] = cells.astype(BF)
        slot = pl.ds(pl.multiple_of(col * 32, 32), 32)

        @pl.when(n < 7)
        def _():
            push(pool.at[n], got_pool.at[slot], pool_out, pool_in, (row, c))

        @pl.when(n == 7)
        def _():
            got_pool[slot, :] = pool[n]

    steps = (exchange(stack1, stack2, 1), exchange(stack2, stack3, 2), step3, step4)

    def slot(u, carry):
        @pl.when(u == 1)
        def _():
            outer_rows()

        @pl.when(u < 3)
        def _():
            taps(u)

        @pl.when((u >= 3) & (u < 3 + STRIPS))
        def _():
            strip(u - 3)

        for step, (first, second, third) in zip(steps, WHEN):
            @pl.when((u == first) | (u == second) | (u == third))
            def _():
                g = jnp.where(u == first, 0, jnp.where(u == second, 1, 2))
                step(g, first_tap(g))

        return carry

    lax.fori_loop(0, WHEN[-1][-1] + 1, slot, 0)

    arrived(got_pool.at[pl.ds(0, 7 * 32)], pool_in)
    gc_ref[...] = got_pool[...]

    arrived(pool.at[pl.ds(0, 7)], pool_out)
    arrived(got_coarse.at[pl.ds(0, 7)], coarse_out)

    for phase, count in enumerate((7, 3, 3, 7)):
        arrived(dcat.at[pl.ds(0, 9 * count * PIECE // 3)], ar_out.at[phase])


def store_kernel(gf_ref, gc_ref, gw_ref, gf_out, gc_out, gw_out, sem):
    pairs = [(gw_ref.at[t], gw_out.at[t]) for t in range(9)]
    for n in range(8):
        some = pl.ds(n * (PIX // 8), PIX // 8)
        pairs.append((gf_ref.at[some], gf_out.at[some]))
    pairs.append((gc_ref, gc_out))
    copies = [pltpu.make_async_copy(*pair, sem.at[n]) for n, pair in enumerate(pairs)]
    for copy in copies:
        copy.start()
    for copy in copies:
        copy.wait()


def per_device(fine_input, coarse_feat, conv_weight, step_scale, timesteps, cotangent):
    anywhere = pl.BlockSpec(memory_space=pl.ANY)
    vmem = pl.BlockSpec(memory_space=pltpu.VMEM)
    buf = pltpu.VMEM
    dma = pltpu.SemaphoreType.DMA
    def in_hbm(array, shape):
        return pltpu.with_memory_space_constraint(array.reshape(shape), pltpu.HBM)

    results = pl.pallas_call(
        fused_kernel,
        name="fused",
        out_shape=(
            pltpu.VMEM((PIX, C), BF),
            pltpu.VMEM((C, C), BF),
            pltpu.VMEM((9, C, C), F32),
        ),
        in_specs=[pl.BlockSpec(memory_space=pltpu.SMEM)] + [anywhere] * 5,
        out_specs=(vmem, vmem, vmem),
        scratch_shapes=[
            buf((1000, C), F32),
            buf((ROWS, COLS, C), BF),
            buf((ROWS, COLS, C), BF),
            buf((C, C), BF),
            buf((9, C, C), BF),
            buf((3, 3 * C, C), BF),
            buf(((ROWS + 2) * COLS, 3 * C), BF),
            buf((C, PIX), BF),
            buf((PIX, C), F32),
            buf((2, ROWS, C), F32),
            buf((2, ROWS, C), BF),
            buf((2, ROWS, C), BF),
            buf((2, COLS, C), BF),
            buf((4, 16, C), BF),
            buf((8, 32, C), BF),
            buf((2, COLS, 128), F32),
            buf((2, ROWS, C), F32),
            buf((8, 32, C), BF),
            buf((C, C), BF),
            buf((9, C, C), BF),
            buf((9, 8, PIECE, C), BF),
            buf((9, 4, PIECE, C), BF),
            buf((9, 4, PIECE, C), BF),
            buf((9, C, C), BF),
            buf((2, COLS, 128), F32),
            dma((5,)),
            dma((8,)),
            dma((8,)),
            dma,
            dma((8,)),
            dma,
            dma,
            dma((4,)),
            dma((4, 3)),
        ],
        compiler_params=pltpu.CompilerParams(
            collective_id=0, has_side_effects=True, vmem_limit_bytes=40 * 2**20
        ),
        cost_estimate=pl.CostEstimate(
            flops=2 * 2 * 9 * PIX * C * C, bytes_accessed=12 * 2**20, transcendentals=PIX * C
        ),
    )(
        timesteps,
        in_hbm(step_scale, step_scale.shape),
        in_hbm(fine_input, (ROWS, COLS, C)),
        in_hbm(coarse_feat, (C, C)),
        in_hbm(conv_weight, (9, C, C)),
        in_hbm(cotangent, (ROWS, COLS, C)),
    )
    gf, gc, gw = pl.pallas_call(
        store_kernel,
        name="store",
        out_shape=(
            jax.ShapeDtypeStruct((PIX, C), BF),
            jax.ShapeDtypeStruct((C, C), BF),
            jax.ShapeDtypeStruct((9, C, C), F32),
        ),
        in_specs=[vmem] * 3,
        out_specs=(anywhere, anywhere, anywhere),
        scratch_shapes=[dma((18,))],
        compiler_params=pltpu.CompilerParams(vmem_limit_bytes=2**20),
    )(*(pltpu.with_memory_space_constraint(result, pltpu.VMEM) for result in results))
    return gf.reshape(1, ROWS, COLS, C), gc.reshape(1, 1, C, C), gw.reshape(3, 3, C, C)


def solution(mesh):
    return jax.shard_map(
        per_device,
        mesh=mesh,
        in_specs=(
            P(None, "row", "col", None),
            P(None, ("row", "col"), None, None),
            P(),
            P(),
            P(),
            P(None, "row", "col", None),
        ),
        out_specs=(P(None, "row", "col", None), P(None, ("row", "col"), None, None), P()),
        check_vma=False,
    )
```

```python
import functools
import math

import jax
import jax.numpy as jnp
from jax import lax
from jax.experimental import pallas as pl
from jax.experimental.pallas import tpu as pltpu
from jax.sharding import PartitionSpec as P

MESH = pl.DeviceIdType.MESH
BF = jnp.bfloat16
F32 = jnp.float32
TN = (((0,), (0,)), ((), ()))
ROWS, COLS, C = 32, 128, 256
PIX = ROWS * COLS
GRID = (16, 8)
STRIPS = 8
PIECE = C // 8
WHEN = ((2, 4, 6), (6, 8, 9), (10, 11, 12), (14, 15, 16))


def place(x, y, z, k):
    return (y * 4 + (z // 2) * 2 + k, (z % 2) * 4 + x)


def other(axis, d, flip, x, y, z, k):
    at = [x, y, z]
    at[axis] = (at[axis] + d) % 4
    return place(*at, (k + flip) % 2)


def fused_kernel(
    ts, ss_hbm, fine_hbm, coarse_hbm, w_hbm, cot_hbm,
    gf_ref, gc_ref, gw_ref,
    ss, cot, fine, coarse, w, wcat, dcat, act, slope,
    edge32, edge, got_edge, got_row, got_corner, got_coarse, up, patch,
    pool, got_pool, part, stack1, stack2, stack3, whole, pooled_rows,
    load_sem, out_sem, in_sem, coarse_out, coarse_in, pool_out, pool_in, ar_out, ar_in,
):
    row, col = lax.axis_index("row"), lax.axis_index("col")
    y, z_hi, k, z_lo, x = row // 4, (row // 2) % 2, row % 2, col // 4, col % 4
    z = z_hi * 2 + z_lo
    here = (x, y, z, k)

    down, upw, right, left = (row + 1) % 16, (row + 15) % 16, (col + 1) % 8, (col + 7) % 8
    partners = [(row, (col + d) % 8) for d in range(1, 8)]
    partners += [(down, col), (upw, col)]
    partners += [(a, b) for a in (down, upw) for b in (left, right)]
    partners += [other(1, d, 0, *here) for d in range(1, 4)]
    partners += [place(x, y, (z + 2) % 4, k), place(x, y, 3 - z, k)]
    partners += [other(axis, d, 1, *here) for axis in range(3) for d in range(1, 4)]
    barrier = pltpu.get_barrier_semaphore()
    for partner in partners:
        pl.semaphore_signal(barrier, inc=1, device_id=partner, device_id_type=MESH)

    loads = [
        pltpu.make_async_copy(src, dst, load_sem.at[n])
        for n, (src, dst) in enumerate(
            (
                (coarse_hbm, coarse), (cot_hbm, cot),
                (ss_hbm, ss), (w_hbm, w), (fine_hbm, fine),
            )
        )
    ]
    for copy in loads:
        copy.start()

    def push(src, dst, send, recv, to):
        copy = pltpu.make_async_remote_copy(
            src_ref=src, dst_ref=dst, send_sem=send, recv_sem=recv,
            device_id=to, device_id_type=MESH,
        )
        copy.start()
        return copy

    def near_strip(n):
        m = n % 4
        return ((z_lo + n // 4) % 2) * 4 + (x + (m * (m + 1) // 2)) % 4

    loads[0].wait()
    pl.semaphore_wait(barrier, len(partners))
    for n in range(7, 0, -1):
        to = near_strip(n)
        push(
            coarse.at[pl.ds(pl.multiple_of(to * 32, 32), 32)], got_coarse.at[col],
            coarse_out, coarse_in.at[col], (row, to),
        )

    loads[1].wait()

    def take_edge(r, carry):
        edge32[0, pl.ds(r, 1), :] = cot[r, 0:16, :].astype(F32)[0:1]
        edge32[1, pl.ds(r, 1), :] = cot[r, COLS - 16 : COLS, :].astype(F32)[15:16]
        return carry

    lax.fori_loop(0, ROWS, take_edge, 0, unroll=8)
    edge[...] = edge32[...].astype(BF)
    sent = [
        push(edge.at[1], got_edge.at[0], out_sem.at[0], in_sem.at[0], (row, right)),
        push(edge.at[0], got_edge.at[1], out_sem.at[1], in_sem.at[1], (row, left)),
    ]
    sent.append(push(cot.at[ROWS - 1], got_row.at[0], out_sem.at[2], in_sem.at[2], (down, col)))
    sent.append(push(cot.at[0], got_row.at[1], out_sem.at[3], in_sem.at[3], (upw, col)))
    for n, (src_row, first, to) in enumerate(
        (
            (ROWS - 1, COLS - 16, (down, right)),
            (ROWS - 1, 0, (down, left)),
            (0, COLS - 16, (upw, right)),
            (0, 0, (upw, left)),
        )
    ):
        sent.append(
            push(
                cot.at[src_row, pl.ds(first, 16)], got_corner.at[n],
                out_sem.at[4 + n], in_sem.at[4 + n], to,
            )
        )

    loads[2].wait()
    picked = ss[pl.ds(ts[0], 1), :]

    def scaled(raw):
        return (raw.astype(F32) * picked).astype(BF)

    def shift_row(r, carry):
        mid = scaled(cot[r])
        wide = mid.astype(F32)
        at = pl.ds(pl.multiple_of((r + 1) * COLS, COLS), COLS)
        dcat[at, C : 2 * C] = mid
        dcat[at, 2 * C : 3 * C] = pltpu.roll(wide, 1, 0).astype(BF)
        dcat[at, 0:C] = pltpu.roll(wide, COLS - 1, 0).astype(BF)
        return carry

    lax.fori_loop(0, ROWS, shift_row, 0, unroll=2)

    loads[3].wait()

    def turn_weight(i, carry):
        for j in range(3):
            wcat[i, j * C : (j + 1) * C, :] = w[3 * i + j].T
        return carry

    lax.fori_loop(0, 3, turn_weight, 0)

    loads[4].wait()

    def activate(n, carry):
        strip = near_strip(n)

        @pl.when(n == 0)
        def _():
            got_coarse[strip] = coarse[pl.ds(pl.multiple_of(strip * 32, 32), 32), :]

        @pl.when(n > 0)
        def _():
            some = got_coarse.at[strip]
            pltpu.make_async_copy(some, some, coarse_in.at[strip]).wait()

        cells = got_coarse[strip].astype(F32)
        for q in range(4):
            for half in range(2):
                up[half, pl.ds(q, 32, stride=4), :] = cells[:, half * 128 : half * 128 + 128]

        def fine_row(q, carry):
            r = strip * 4 + q
            hidden = fine[r].astype(F32) + jnp.concatenate([up[0], up[1]], axis=1)
            sig = 0.5 * jnp.tanh(0.5 * hidden) + 0.5
            value = hidden * sig
            at = pl.ds(pl.multiple_of(r * COLS, COLS), COLS)
            act[at, :] = value.astype(BF)
            slope[at, :] = sig + value * (1.0 - sig)
            return carry

        return lax.fori_loop(0, 4, fine_row, carry, unroll=2)

    lax.fori_loop(0, STRIPS, activate, 0)

    keep_top = jnp.where(row > 0, 1.0, 0.0)
    keep_bottom = jnp.where(row < 15, 1.0, 0.0)
    keep_left = jnp.where(col > 0, 1.0, 0.0)
    keep_right = jnp.where(col < 7, 1.0, 0.0)

    for copy in sent[:2]:
        copy.wait()
    patch[0] = scaled(got_edge[0]).astype(F32) * keep_left
    patch[1] = scaled(got_edge[1]).astype(F32) * keep_right
    spot = lax.broadcasted_iota(jnp.int32, (16, C), 0)

    def patch_row(r, carry):
        first = pl.ds(pl.multiple_of((r + 1) * COLS, COLS), 16)
        last = pl.ds(pl.multiple_of((r + 1) * COLS + COLS - 16, 16), 16)
        lo = dcat[first, 2 * C : 3 * C].astype(F32)
        dcat[first, 2 * C : 3 * C] = jnp.where(spot == 0, patch[0, pl.ds(r, 1), :], lo).astype(BF)
        hi = dcat[last, 0:C].astype(F32)
        dcat[last, 0:C] = jnp.where(spot == 15, patch[1, pl.ds(r, 1), :], hi).astype(BF)
        return carry

    lax.fori_loop(0, ROWS, patch_row, 0, unroll=4)
    spot_row = lax.broadcasted_iota(jnp.int32, (COLS, C), 0)

    def outer_rows():
        for copy in sent[2:]:
            copy.wait()
        for n, (start, keep) in enumerate(((0, keep_top), ((ROWS + 1) * COLS, keep_bottom))):
            wide = scaled(got_row[n]).astype(F32) * keep
            near = scaled(got_corner[2 * n]).astype(F32)[15:16] * (keep * keep_left)
            far = scaled(got_corner[2 * n + 1]).astype(F32)[0:1] * (keep * keep_right)
            at = pl.ds(start, COLS)
            dcat[at, C : 2 * C] = wide.astype(BF)
            dcat[at, 2 * C : 3 * C] = jnp.where(
                spot_row == 0, near, pltpu.roll(wide, 1, 0)
            ).astype(BF)
            dcat[at, 0:C] = jnp.where(
                spot_row == COLS - 1, far, pltpu.roll(wide, COLS - 1, 0)
            ).astype(BF)

    def mine(axis):
        return here[axis] * 2 + k

    def eight(axis):
        return [
            (((here[axis] + d) % 4) * 2 + (k + flip) % 2, other(axis, d, flip, *here))
            for d, flip in ((2, 1), (2, 0), (1, 1), (3, 1), (1, 0), (3, 0), (0, 1))
        ]

    def peers(axis):
        return [other(axis, d, 0, *here) for d in (2, 1, 3)]

    def arrived(some, sem):
        pltpu.make_async_copy(some, some, sem).wait()

    def total(stack, t):
        out = stack[t, 0].astype(F32)
        for n in range(1, stack.shape[1]):
            out = out + stack[t, n].astype(F32)
        return out.astype(BF)

    def quarter(m):
        return pl.ds(pl.multiple_of(m * PIECE, PIECE), PIECE)

    def three(stack, first, rows):
        return stack.at[pl.ds(first, 3), pl.ds(0, rows)]

    def exchange(before, after, phase):
        def step(g, first):
            arrived(three(before, first, before.shape[1] - 1), ar_in.at[phase - 1, g])
            for j in range(3):
                after[first + j, here[(j + phase) % 3]] = total(before, first + j)
            for j in range(3):
                t, axis = first + j, (j + phase) % 3
                for to in peers(axis):
                    push(
                        after.at[t, here[axis]], after.at[t, here[axis]],
                        ar_out.at[phase], ar_in.at[phase, g], to,
                    )

        return step

    def step3(g, first):
        arrived(three(stack3, first, 3), ar_in.at[2, g])
        for j in range(3):
            whole[first + j, quarter(mine(j)), :] = total(stack3, first + j)
        for j in range(3):
            some = whole.at[first + j, quarter(mine(j))]
            for _, to in eight(j):
                push(some, some, ar_out.at[3], ar_in.at[3, g], to)

    scale = 1.0 / math.sqrt(PIX * GRID[0] * GRID[1])

    def step4(g, first):
        arrived(three(whole, first, 7 * PIECE), ar_in.at[3, g])
        for j in range(3):
            gw_ref[first + j] = whole[first + j].astype(F32) * scale

    def first_tap(g):
        return 3 * ((4 - g) % 3)

    def taps(g):
        first = first_tap(g)
        at = pl.ds(pl.multiple_of(2 * COLS - first // 3 * COLS, COLS), PIX)
        row_of_taps = lax.dot_general(act[...], dcat[at, :], TN, preferred_element_type=F32)
        for j in range(3):
            part[first + j] = row_of_taps[:, j * C : (j + 1) * C].astype(BF)
        for j in range(3):
            t = first + j
            for m, to in eight(j):
                push(part.at[t, quarter(m)], stack1.at[t, mine(j)], ar_out.at[0], ar_in.at[0, g], to)
            stack1[t, mine(j)] = part[t, quarter(mine(j)), :]

    def strip(n):
        c = (col + 1 + n) % 8
        base = c * (4 * COLS)
        acc = None
        for i in range(3):
            at = pl.ds(pl.multiple_of(base + (2 - i) * COLS, COLS), 4 * COLS)
            term = jnp.dot(dcat[at, :], wcat[i], preferred_element_type=F32)
            acc = term if acc is None else acc + term
        at = pl.ds(pl.multiple_of(base, COLS), 4 * COLS)
        dh = acc * slope[at, :]
        gf_ref[at, :] = dh.astype(BF)
        tall = dh[0:COLS] + dh[COLS : 2 * COLS] + dh[2 * COLS : 3 * COLS] + dh[3 * COLS :]
        for half in range(2):
            lanes = slice(half * 128, half * 128 + 128)
            pooled_rows[half] = tall[:, lanes]
            cells = pooled_rows[half, pl.ds(0, 32, stride=4), :]
            for q in range(1, 4):
                cells = cells + pooled_rows[half, pl.ds(q, 32, stride=4), :]
            pool[n, :, lanes] = cells.astype(BF)
        slot = pl.ds(pl.multiple_of(col * 32, 32), 32)

        @pl.when(n < 7)
        def _():
            push(pool.at[n], got_pool.at[slot], pool_out, pool_in, (row, c))

        @pl.when(n == 7)
        def _():
            got_pool[slot, :] = pool[n]

    steps = (exchange(stack1, stack2, 1), exchange(stack2, stack3, 2), step3, step4)

    def slot(u, carry):
        @pl.when(u == 1)
        def _():
            outer_rows()

        @pl.when(u < 3)
        def _():
            taps(u)

        @pl.when((u >= 3) & (u < 3 + STRIPS))
        def _():
            strip(u - 3)

        for step, (first, second, third) in zip(steps, WHEN):
            @pl.when((u == first) | (u == second) | (u == third))
            def _():
                g = jnp.where(u == first, 0, jnp.where(u == second, 1, 2))
                step(g, first_tap(g))

        return carry

    lax.fori_loop(0, WHEN[-1][-1] + 1, slot, 0)

    arrived(got_pool.at[pl.ds(0, 7 * 32)], pool_in)
    gc_ref[...] = got_pool[...]

    arrived(pool.at[pl.ds(0, 7)], pool_out)
    arrived(got_coarse.at[pl.ds(0, 7)], coarse_out)

    for phase, count in enumerate((7, 3, 3, 7)):
        arrived(dcat.at[pl.ds(0, 9 * count * PIECE // 3)], ar_out.at[phase])


def store_kernel(gf_ref, gc_ref, gw_ref, gf_out, gc_out, gw_out, sem):
    pairs = [(gw_ref.at[t], gw_out.at[t]) for t in range(9)]
    for n in range(8):
        some = pl.ds(n * (PIX // 8), PIX // 8)
        pairs.append((gf_ref.at[some], gf_out.at[some]))
    pairs.append((gc_ref, gc_out))
    copies = [pltpu.make_async_copy(*pair, sem.at[n]) for n, pair in enumerate(pairs)]
    for copy in copies:
        copy.start()
    for copy in copies:
        copy.wait()


def per_device(fine_input, coarse_feat, conv_weight, step_scale, timesteps, cotangent):
    anywhere = pl.BlockSpec(memory_space=pl.ANY)
    vmem = pl.BlockSpec(memory_space=pltpu.VMEM)
    buf = pltpu.VMEM
    dma = pltpu.SemaphoreType.DMA
    def in_hbm(array, shape):
        return pltpu.with_memory_space_constraint(array.reshape(shape), pltpu.HBM)

    results = pl.pallas_call(
        fused_kernel,
        name="fused",
        out_shape=(
            pltpu.VMEM((PIX, C), BF),
            pltpu.VMEM((C, C), BF),
            pltpu.VMEM((9, C, C), F32),
        ),
        in_specs=[pl.BlockSpec(memory_space=pltpu.SMEM)] + [anywhere] * 5,
        out_specs=(vmem, vmem, vmem),
        scratch_shapes=[
            buf((1000, C), F32),
            buf((ROWS, COLS, C), BF),
            buf((ROWS, COLS, C), BF),
            buf((C, C), BF),
            buf((9, C, C), BF),
            buf((3, 3 * C, C), BF),
            buf(((ROWS + 2) * COLS, 3 * C), BF),
            buf((PIX, C), BF),
            buf((PIX, C), F32),
            buf((2, ROWS, C), F32),
            buf((2, ROWS, C), BF),
            buf((2, ROWS, C), BF),
            buf((2, COLS, C), BF),
            buf((4, 16, C), BF),
            buf((8, 32, C), BF),
            buf((2, COLS, 128), F32),
            buf((2, ROWS, C), F32),
            buf((8, 32, C), BF),
            buf((C, C), BF),
            buf((9, C, C), BF),
            buf((9, 8, PIECE, C), BF),
            buf((9, 4, PIECE, C), BF),
            buf((9, 4, PIECE, C), BF),
            buf((9, C, C), BF),
            buf((2, COLS, 128), F32),
            dma((5,)),
            dma((8,)),
            dma((8,)),
            dma,
            dma((8,)),
            dma,
            dma,
            dma((4,)),
            dma((4, 3)),
        ],
        compiler_params=pltpu.CompilerParams(
            collective_id=0, has_side_effects=True, vmem_limit_bytes=40 * 2**20
        ),
        cost_estimate=pl.CostEstimate(
            flops=2 * 2 * 9 * PIX * C * C, bytes_accessed=12 * 2**20, transcendentals=PIX * C
        ),
    )(
        timesteps,
        in_hbm(step_scale, step_scale.shape),
        in_hbm(fine_input, (ROWS, COLS, C)),
        in_hbm(coarse_feat, (C, C)),
        in_hbm(conv_weight, (9, C, C)),
        in_hbm(cotangent, (ROWS, COLS, C)),
    )
    gf, gc, gw = pl.pallas_call(
        store_kernel,
        name="store",
        out_shape=(
            jax.ShapeDtypeStruct((PIX, C), BF),
            jax.ShapeDtypeStruct((C, C), BF),
            jax.ShapeDtypeStruct((9, C, C), F32),
        ),
        in_specs=[vmem] * 3,
        out_specs=(anywhere, anywhere, anywhere),
        scratch_shapes=[dma((18,))],
        compiler_params=pltpu.CompilerParams(vmem_limit_bytes=2**20),
    )(*(pltpu.with_memory_space_constraint(result, pltpu.VMEM) for result in results))
    return gf.reshape(1, ROWS, COLS, C), gc.reshape(1, 1, C, C), gw.reshape(3, 3, C, C)


def solution(mesh):
    return jax.shard_map(
        per_device,
        mesh=mesh,
        in_specs=(
            P(None, "row", "col", None),
            P(None, ("row", "col"), None, None),
            P(),
            P(),
            P(),
            P(None, "row", "col", None),
        ),
        out_specs=(P(None, "row", "col", None), P(None, ("row", "col"), None, None), P()),
        check_vma=False,
    )
```

```python
import functools
import math

import jax
import jax.numpy as jnp
from jax import lax
from jax.experimental import pallas as pl
from jax.experimental.pallas import tpu as pltpu
from jax.sharding import PartitionSpec as P

MESH = pl.DeviceIdType.MESH
BF = jnp.bfloat16
F32 = jnp.float32
TN = (((0,), (0,)), ((), ()))
ROWS, COLS, C = 32, 128, 256
PIX = ROWS * COLS
GRID = (16, 8)
STRIPS = 8
PIECE = C // 8
WHEN = ((3, 4, 5), (6, 7, 8), (8, 9, 11), (12, 13, 14))


def place(x, y, z, k):
    return (y * 4 + (z // 2) * 2 + k, (z % 2) * 4 + x)


def other(axis, d, flip, x, y, z, k):
    at = [x, y, z]
    at[axis] = (at[axis] + d) % 4
    return place(*at, (k + flip) % 2)


def fused_kernel(
    ts, ss_hbm, fine_hbm, coarse_hbm, w_hbm, cot_hbm,
    gf_ref, gc_ref, gw_ref,
    ss, cot, fine, coarse, w, wcat, dcat, act, slope,
    rim, edge32, edge, got_edge, got_row, got_corner, got_coarse, up, patch,
    pool, got_pool, part, stack1, stack2, stack3, whole, pooled_rows,
    load_sem, out_sem, in_sem, coarse_out, coarse_in, pool_out, pool_in, ar_out, ar_in,
):
    row, col = lax.axis_index("row"), lax.axis_index("col")
    y, z_hi, k, z_lo, x = row // 4, (row // 2) % 2, row % 2, col // 4, col % 4
    z = z_hi * 2 + z_lo
    here = (x, y, z, k)

    down, upw, right, left = (row + 1) % 16, (row + 15) % 16, (col + 1) % 8, (col + 7) % 8
    partners = [(row, (col + d) % 8) for d in range(1, 8)]
    partners += [(down, col), (upw, col)]
    partners += [(a, b) for a in (down, upw) for b in (left, right)]
    partners += [other(1, d, 0, *here) for d in range(1, 4)]
    partners += [place(x, y, (z + 2) % 4, k), place(x, y, 3 - z, k)]
    partners += [other(axis, d, 1, *here) for axis in range(3) for d in range(1, 4)]
    barrier = pltpu.get_barrier_semaphore()
    for partner in partners:
        pl.semaphore_signal(barrier, inc=1, device_id=partner, device_id_type=MESH)

    loads = [
        pltpu.make_async_copy(src, dst, load_sem.at[n])
        for n, (src, dst) in enumerate(
            (
                (coarse_hbm, coarse), (cot_hbm.at[:, pl.ds(0, 16)], rim.at[0]),
                (cot_hbm.at[:, pl.ds(COLS - 16, 16)], rim.at[1]), (cot_hbm, cot),
                (ss_hbm, ss), (w_hbm, w), (fine_hbm, fine),
            )
        )
    ]
    for copy in loads[:4]:
        copy.start()

    def push(src, dst, send, recv, to):
        copy = pltpu.make_async_remote_copy(
            src_ref=src, dst_ref=dst, send_sem=send, recv_sem=recv,
            device_id=to, device_id_type=MESH,
        )
        copy.start()
        return copy

    def near_strip(n):
        m = n % 4
        return ((z_lo + n // 4) % 2) * 4 + (x + (m * (m + 1) // 2)) % 4

    loads[0].wait()
    pl.semaphore_wait(barrier, len(partners))
    for n in range(7, 0, -1):
        to = near_strip(n)
        push(
            coarse.at[pl.ds(pl.multiple_of(to * 32, 32), 32)], got_coarse.at[col],
            coarse_out, coarse_in.at[col], (row, to),
        )

    for copy in loads[4:]:
        copy.start()

    loads[1].wait()
    loads[2].wait()

    def take_edge(r, carry):
        edge32[0, pl.ds(r, 1), :] = rim[0, r].astype(F32)[0:1]
        edge32[1, pl.ds(r, 1), :] = rim[1, r].astype(F32)[15:16]
        return carry

    lax.fori_loop(0, ROWS, take_edge, 0)
    edge[...] = edge32[...].astype(BF)
    sent = [
        push(edge.at[1], got_edge.at[0], out_sem.at[0], in_sem.at[0], (row, right)),
        push(edge.at[0], got_edge.at[1], out_sem.at[1], in_sem.at[1], (row, left)),
    ]
    loads[3].wait()
    sent.append(push(cot.at[ROWS - 1], got_row.at[0], out_sem.at[2], in_sem.at[2], (down, col)))
    sent.append(push(cot.at[0], got_row.at[1], out_sem.at[3], in_sem.at[3], (upw, col)))
    for n, (src_row, first, to) in enumerate(
        (
            (ROWS - 1, COLS - 16, (down, right)),
            (ROWS - 1, 0, (down, left)),
            (0, COLS - 16, (upw, right)),
            (0, 0, (upw, left)),
        )
    ):
        sent.append(
            push(
                cot.at[src_row, pl.ds(first, 16)], got_corner.at[n],
                out_sem.at[4 + n], in_sem.at[4 + n], to,
            )
        )

    loads[4].wait()
    picked = ss[pl.ds(ts[0], 1), :]

    def scaled(raw):
        return (raw.astype(F32) * picked).astype(BF)

    def shift_row(r, carry):
        mid = scaled(cot[r])
        wide = mid.astype(F32)
        at = pl.ds(pl.multiple_of((r + 1) * COLS, COLS), COLS)
        dcat[at, C : 2 * C] = mid
        dcat[at, 2 * C : 3 * C] = pltpu.roll(wide, 1, 0).astype(BF)
        dcat[at, 0:C] = pltpu.roll(wide, COLS - 1, 0).astype(BF)
        return carry

    lax.fori_loop(0, ROWS, shift_row, 0)

    loads[5].wait()

    def turn_weight(i, carry):
        for j in range(3):
            wcat[i, j * C : (j + 1) * C, :] = w[3 * i + j].T
        return carry

    lax.fori_loop(0, 3, turn_weight, 0)

    loads[6].wait()

    def activate(n, carry):
        strip = near_strip(n)

        @pl.when(n == 0)
        def _():
            got_coarse[strip] = coarse[pl.ds(pl.multiple_of(strip * 32, 32), 32), :]

        @pl.when(n > 0)
        def _():
            some = got_coarse.at[strip]
            pltpu.make_async_copy(some, some, coarse_in.at[strip]).wait()

        cells = got_coarse[strip].astype(F32)
        for q in range(4):
            for half in range(2):
                up[half, pl.ds(q, 32, stride=4), :] = cells[:, half * 128 : half * 128 + 128]

        def fine_row(q, carry):
            r = strip * 4 + q
            hidden = fine[r].astype(F32) + jnp.concatenate([up[0], up[1]], axis=1)
            sig = 0.5 * jnp.tanh(0.5 * hidden) + 0.5
            value = hidden * sig
            at = pl.ds(pl.multiple_of(r * COLS, COLS), COLS)
            act[at, :] = value.astype(BF)
            slope[at, :] = sig + value * (1.0 - sig)
            return carry

        return lax.fori_loop(0, 4, fine_row, carry)

    lax.fori_loop(0, STRIPS, activate, 0)

    keep_top = jnp.where(row > 0, 1.0, 0.0)
    keep_bottom = jnp.where(row < 15, 1.0, 0.0)
    keep_left = jnp.where(col > 0, 1.0, 0.0)
    keep_right = jnp.where(col < 7, 1.0, 0.0)

    for copy in sent[:2]:
        copy.wait()
    patch[0] = scaled(got_edge[0]).astype(F32) * keep_left
    patch[1] = scaled(got_edge[1]).astype(F32) * keep_right
    spot = lax.broadcasted_iota(jnp.int32, (16, C), 0)

    def patch_row(r, carry):
        first = pl.ds(pl.multiple_of((r + 1) * COLS, COLS), 16)
        last = pl.ds(pl.multiple_of((r + 1) * COLS + COLS - 16, 16), 16)
        lo = dcat[first, 2 * C : 3 * C].astype(F32)
        dcat[first, 2 * C : 3 * C] = jnp.where(spot == 0, patch[0, pl.ds(r, 1), :], lo).astype(BF)
        hi = dcat[last, 0:C].astype(F32)
        dcat[last, 0:C] = jnp.where(spot == 15, patch[1, pl.ds(r, 1), :], hi).astype(BF)
        return carry

    lax.fori_loop(0, ROWS, patch_row, 0)
    spot_row = lax.broadcasted_iota(jnp.int32, (COLS, C), 0)

    def outer_rows():
        for copy in sent[2:]:
            copy.wait()
        for n, (start, keep) in enumerate(((0, keep_top), ((ROWS + 1) * COLS, keep_bottom))):
            wide = scaled(got_row[n]).astype(F32) * keep
            near = scaled(got_corner[2 * n]).astype(F32)[15:16] * (keep * keep_left)
            far = scaled(got_corner[2 * n + 1]).astype(F32)[0:1] * (keep * keep_right)
            at = pl.ds(start, COLS)
            dcat[at, C : 2 * C] = wide.astype(BF)
            dcat[at, 2 * C : 3 * C] = jnp.where(
                spot_row == 0, near, pltpu.roll(wide, 1, 0)
            ).astype(BF)
            dcat[at, 0:C] = jnp.where(
                spot_row == COLS - 1, far, pltpu.roll(wide, COLS - 1, 0)
            ).astype(BF)

    def mine(axis):
        return here[axis] * 2 + k

    def eight(axis):
        return [
            (((here[axis] + d) % 4) * 2 + (k + flip) % 2, other(axis, d, flip, *here))
            for d, flip in ((2, 1), (2, 0), (1, 1), (3, 1), (1, 0), (3, 0), (0, 1))
        ]

    def peers(axis):
        return [other(axis, d, 0, *here) for d in (2, 1, 3)]

    def arrived(some, sem):
        pltpu.make_async_copy(some, some, sem).wait()

    def total(stack, t):
        out = stack[t, 0].astype(F32)
        for n in range(1, stack.shape[1]):
            out = out + stack[t, n].astype(F32)
        return out.astype(BF)

    def quarter(m):
        return pl.ds(pl.multiple_of(m * PIECE, PIECE), PIECE)

    def three(stack, first, rows):
        return stack.at[pl.ds(first, 3), pl.ds(0, rows)]

    def exchange(before, after, phase):
        def step(g, first):
            arrived(three(before, first, before.shape[1] - 1), ar_in.at[phase - 1, g])
            for j in range(3):
                after[first + j, here[(j + phase) % 3]] = total(before, first + j)
            for n in range(3):
                for j in range(3):
                    t, axis = first + j, (j + phase) % 3
                    push(
                        after.at[t, here[axis]], after.at[t, here[axis]],
                        ar_out.at[phase], ar_in.at[phase, g], peers(axis)[n],
                    )

        return step

    def step3(g, first):
        arrived(three(stack3, first, 3), ar_in.at[2, g])
        for j in range(3):
            whole[first + j, quarter(mine(j)), :] = total(stack3, first + j)
        for n in range(7):
            for j in range(3):
                some = whole.at[first + j, quarter(mine(j))]
                push(some, some, ar_out.at[3], ar_in.at[3, g], eight(j)[n][1])

    scale = 1.0 / math.sqrt(PIX * GRID[0] * GRID[1])

    def step4(g, first):
        arrived(three(whole, first, 7 * PIECE), ar_in.at[3, g])
        for j in range(3):
            gw_ref[first + j] = whole[first + j].astype(F32) * scale

    def first_tap(g):
        return 3 * ((4 - g) % 3)

    def taps(g):
        first = first_tap(g)
        at = pl.ds(pl.multiple_of(2 * COLS - first // 3 * COLS, COLS), PIX)
        row_of_taps = lax.dot_general(act[...], dcat[at, :], TN, preferred_element_type=F32)
        for j in range(3):
            part[first + j] = row_of_taps[:, j * C : (j + 1) * C].astype(BF)
        for n in range(7):
            for j in range(3):
                t = first + j
                m, to = eight(j)[n]
                push(part.at[t, quarter(m)], stack1.at[t, mine(j)], ar_out.at[0], ar_in.at[0, g], to)
        for j in range(3):
            stack1[first + j, mine(j)] = part[first + j, quarter(mine(j)), :]

    def strip(n):
        c = (col + 1 + n) % 8
        base = c * (4 * COLS)
        acc = None
        for i in range(3):
            at = pl.ds(pl.multiple_of(base + (2 - i) * COLS, COLS), 4 * COLS)
            term = jnp.dot(dcat[at, :], wcat[i], preferred_element_type=F32)
            acc = term if acc is None else acc + term
        at = pl.ds(pl.multiple_of(base, COLS), 4 * COLS)
        dh = acc * slope[at, :]
        gf_ref[at, :] = dh.astype(BF)
        tall = dh[0:COLS] + dh[COLS : 2 * COLS] + dh[2 * COLS : 3 * COLS] + dh[3 * COLS :]
        for half in range(2):
            lanes = slice(half * 128, half * 128 + 128)
            pooled_rows[half] = tall[:, lanes]
            cells = pooled_rows[half, pl.ds(0, 32, stride=4), :]
            for q in range(1, 4):
                cells = cells + pooled_rows[half, pl.ds(q, 32, stride=4), :]
            pool[n, :, lanes] = cells.astype(BF)
        slot = pl.ds(pl.multiple_of(col * 32, 32), 32)

        @pl.when(n < 7)
        def _():
            push(pool.at[n], got_pool.at[slot], pool_out, pool_in, (row, c))

        @pl.when(n == 7)
        def _():
            got_pool[slot, :] = pool[n]

    steps = (exchange(stack1, stack2, 1), exchange(stack2, stack3, 2), step3, step4)

    def slot(u, carry):
        @pl.when(u == 1)
        def _():
            outer_rows()

        @pl.when(u < 3)
        def _():
            taps(u)

        @pl.when((u >= 3) & (u < 3 + STRIPS))
        def _():
            strip(u - 3)

        for step, (first, second, third) in zip(steps, WHEN):
            @pl.when((u == first) | (u == second) | (u == third))
            def _():
                g = jnp.where(u == first, 0, jnp.where(u == second, 1, 2))
                step(g, first_tap(g))

        return carry

    lax.fori_loop(0, WHEN[-1][-1], slot, 0)

    arrived(got_pool.at[pl.ds(0, 7 * 32)], pool_in)
    gc_ref[...] = got_pool[...]
    arrived(pool.at[pl.ds(0, 7)], pool_out)
    arrived(got_coarse.at[pl.ds(0, 7)], coarse_out)
    for phase, count in enumerate((7, 3, 3, 7)):
        arrived(dcat.at[pl.ds(0, 9 * count * PIECE // 3)], ar_out.at[phase])
    steps[-1](2, first_tap(2))


def store_kernel(gf_ref, gc_ref, gw_ref, gf_out, gc_out, gw_out, sem):
    pairs = [(gw_ref.at[t], gw_out.at[t]) for t in range(9)]
    for n in range(8):
        some = pl.ds(n * (PIX // 8), PIX // 8)
        pairs.append((gf_ref.at[some], gf_out.at[some]))
    pairs.append((gc_ref, gc_out))
    copies = [pltpu.make_async_copy(*pair, sem.at[n]) for n, pair in enumerate(pairs)]
    for copy in copies:
        copy.start()
    for copy in copies:
        copy.wait()


def per_device(fine_input, coarse_feat, conv_weight, step_scale, timesteps, cotangent):
    anywhere = pl.BlockSpec(memory_space=pl.ANY)
    vmem = pl.BlockSpec(memory_space=pltpu.VMEM)
    buf = pltpu.VMEM
    dma = pltpu.SemaphoreType.DMA
    def in_hbm(array, shape):
        return pltpu.with_memory_space_constraint(array.reshape(shape), pltpu.HBM)

    results = pl.pallas_call(
        fused_kernel,
        name="fused",
        out_shape=(
            pltpu.VMEM((PIX, C), BF),
            pltpu.VMEM((C, C), BF),
            pltpu.VMEM((9, C, C), F32),
        ),
        in_specs=[pl.BlockSpec(memory_space=pltpu.SMEM)] + [anywhere] * 5,
        out_specs=(vmem, vmem, vmem),
        scratch_shapes=[
            buf((1000, C), F32),
            buf((ROWS, COLS, C), BF),
            buf((ROWS, COLS, C), BF),
            buf((C, C), BF),
            buf((9, C, C), BF),
            buf((3, 3 * C, C), BF),
            buf(((ROWS + 2) * COLS, 3 * C), BF),
            buf((PIX, C), BF),
            buf((PIX, C), F32),
            buf((2, ROWS, 16, C), BF),
            buf((2, ROWS, C), F32),
            buf((2, ROWS, C), BF),
            buf((2, ROWS, C), BF),
            buf((2, COLS, C), BF),
            buf((4, 16, C), BF),
            buf((8, 32, C), BF),
            buf((2, COLS, 128), F32),
            buf((2, ROWS, C), F32),
            buf((8, 32, C), BF),
            buf((C, C), BF),
            buf((9, C, C), BF),
            buf((9, 8, PIECE, C), BF),
            buf((9, 4, PIECE, C), BF),
            buf((9, 4, PIECE, C), BF),
            buf((9, C, C), BF),
            buf((2, COLS, 128), F32),
            dma((7,)),
            dma((8,)),
            dma((8,)),
            dma,
            dma((8,)),
            dma,
            dma,
            dma((4,)),
            dma((4, 3)),
        ],
        compiler_params=pltpu.CompilerParams(
            collective_id=0, has_side_effects=True, vmem_limit_bytes=40 * 2**20
        ),
        cost_estimate=pl.CostEstimate(
            flops=2 * 2 * 9 * PIX * C * C, bytes_accessed=12 * 2**20, transcendentals=PIX * C
        ),
    )(
        timesteps,
        in_hbm(step_scale, step_scale.shape),
        in_hbm(fine_input, (ROWS, COLS, C)),
        in_hbm(coarse_feat, (C, C)),
        in_hbm(conv_weight, (9, C, C)),
        in_hbm(cotangent, (ROWS, COLS, C)),
    )
    gf, gc, gw = pl.pallas_call(
        store_kernel,
        name="store",
        out_shape=(
            jax.ShapeDtypeStruct((PIX, C), BF),
            jax.ShapeDtypeStruct((C, C), BF),
            jax.ShapeDtypeStruct((9, C, C), F32),
        ),
        in_specs=[vmem] * 3,
        out_specs=(anywhere, anywhere, anywhere),
        scratch_shapes=[dma((18,))],
        compiler_params=pltpu.CompilerParams(vmem_limit_bytes=2**20),
    )(*(pltpu.with_memory_space_constraint(result, pltpu.VMEM) for result in results))
    return gf.reshape(1, ROWS, COLS, C), gc.reshape(1, 1, C, C), gw.reshape(3, 3, C, C)


def solution(mesh):
    return jax.shard_map(
        per_device,
        mesh=mesh,
        in_specs=(
            P(None, "row", "col", None),
            P(None, ("row", "col"), None, None),
            P(),
            P(),
            P(),
            P(None, "row", "col", None),
        ),
        out_specs=(P(None, "row", "col", None), P(None, ("row", "col"), None, None), P()),
        check_vma=False,
    )
```

```python
import functools
import math

import jax
import jax.numpy as jnp
from jax import lax
from jax.experimental import pallas as pl
from jax.experimental.pallas import tpu as pltpu
from jax.sharding import PartitionSpec as P

MESH = pl.DeviceIdType.MESH
BF = jnp.bfloat16
F32 = jnp.float32
TN = (((0,), (0,)), ((), ()))
ROWS, COLS, C = 32, 128, 256
PIX = ROWS * COLS
GRID = (16, 8)
STRIPS = 8
PIECE = C // 8
WHEN = ((3, 4, 5), (6, 7, 8), (8, 9, 11), (12, 13, 14))


def place(x, y, z, k):
    return (y * 4 + (z // 2) * 2 + k, (z % 2) * 4 + x)


def other(axis, d, flip, x, y, z, k):
    at = [x, y, z]
    at[axis] = (at[axis] + d) % 4
    return place(*at, (k + flip) % 2)


def fused_kernel(
    ts, ss_hbm, fine_hbm, coarse_hbm, w_hbm, cot_hbm,
    gf_ref, gc_ref, gw_ref,
    ss, cot, fine, coarse, w, wcat, dcat, act, slope,
    rim, edge32, edge, got_edge, got_row, got_corner, got_coarse, up, patch,
    pool, got_pool, part, stack1, stack2, stack3, whole, pooled_rows,
    load_sem, out_sem, in_sem, coarse_out, coarse_in, pool_out, pool_in, ar_out, ar_in,
):
    row, col = lax.axis_index("row"), lax.axis_index("col")
    y, z_hi, k, z_lo, x = row // 4, (row // 2) % 2, row % 2, col // 4, col % 4
    z = z_hi * 2 + z_lo
    here = (x, y, z, k)

    down, upw, right, left = (row + 1) % 16, (row + 15) % 16, (col + 1) % 8, (col + 7) % 8
    partners = [(row, (col + d) % 8) for d in range(1, 8)]
    partners += [(down, col), (upw, col)]
    partners += [(a, b) for a in (down, upw) for b in (left, right)]
    partners += [other(1, d, 0, *here) for d in range(1, 4)]
    partners += [place(x, y, (z + 2) % 4, k), place(x, y, 3 - z, k)]
    partners += [other(axis, d, 1, *here) for axis in range(3) for d in range(1, 4)]
    barrier = pltpu.get_barrier_semaphore()
    for partner in partners:
        pl.semaphore_signal(barrier, inc=1, device_id=partner, device_id_type=MESH)

    loads = [
        pltpu.make_async_copy(src, dst, load_sem.at[n])
        for n, (src, dst) in enumerate(
            (
                (coarse_hbm, coarse), (cot_hbm.at[:, pl.ds(0, 16)], rim.at[0]),
                (cot_hbm.at[:, pl.ds(COLS - 16, 16)], rim.at[1]), (cot_hbm, cot),
                (ss_hbm, ss), (w_hbm, w), (fine_hbm, fine),
            )
        )
    ]
    for copy in loads[:4]:
        copy.start()

    def push(src, dst, send, recv, to):
        copy = pltpu.make_async_remote_copy(
            src_ref=src, dst_ref=dst, send_sem=send, recv_sem=recv,
            device_id=to, device_id_type=MESH,
        )
        copy.start()
        return copy

    def near_strip(n):
        m = n % 4
        return ((z_lo + n // 4) % 2) * 4 + (x + (m * (m + 1) // 2)) % 4

    loads[0].wait()
    pl.semaphore_wait(barrier, len(partners))
    for n in range(7, 0, -1):
        to = near_strip(n)
        push(
            coarse.at[pl.ds(pl.multiple_of(to * 32, 32), 32)], got_coarse.at[col],
            coarse_out, coarse_in.at[col], (row, to),
        )

    for copy in loads[4:]:
        copy.start()

    loads[1].wait()
    loads[2].wait()

    outer = []
    for n, (side, src_row, to) in enumerate(
        (
            (1, ROWS - 1, (down, right)),
            (0, ROWS - 1, (down, left)),
            (1, 0, (upw, right)),
            (0, 0, (upw, left)),
        )
    ):
        outer.append(
            push(
                rim.at[side, src_row], got_corner.at[n],
                out_sem.at[4 + n], in_sem.at[4 + n], to,
            )
        )

    outer.append(push(cot_hbm.at[ROWS - 1], got_row.at[0], out_sem.at[2], in_sem.at[2], (down, col)))
    outer.append(push(cot_hbm.at[0], got_row.at[1], out_sem.at[3], in_sem.at[3], (upw, col)))

    def take_edge(r, carry):
        edge32[0, pl.ds(r, 1), :] = rim[0, r].astype(F32)[0:1]
        edge32[1, pl.ds(r, 1), :] = rim[1, r].astype(F32)[15:16]
        return carry

    lax.fori_loop(0, ROWS, take_edge, 0)
    edge[...] = edge32[...].astype(BF)
    sent = [
        push(edge.at[1], got_edge.at[0], out_sem.at[0], in_sem.at[0], (row, right)),
        push(edge.at[0], got_edge.at[1], out_sem.at[1], in_sem.at[1], (row, left)),
    ]
    loads[3].wait()

    loads[4].wait()
    picked = ss[pl.ds(ts[0], 1), :]

    def scaled(raw):
        return (raw.astype(F32) * picked).astype(BF)

    def shift_row(r, carry):
        mid = scaled(cot[r])
        wide = mid.astype(F32)
        at = pl.ds(pl.multiple_of((r + 1) * COLS, COLS), COLS)
        dcat[at, C : 2 * C] = mid
        dcat[at, 2 * C : 3 * C] = pltpu.roll(wide, 1, 0).astype(BF)
        dcat[at, 0:C] = pltpu.roll(wide, COLS - 1, 0).astype(BF)
        return carry

    lax.fori_loop(0, ROWS, shift_row, 0)

    loads[5].wait()

    def turn_weight(i, carry):
        for j in range(3):
            wcat[i, j * C : (j + 1) * C, :] = w[3 * i + j].T
        return carry

    lax.fori_loop(0, 3, turn_weight, 0)

    loads[6].wait()

    def activate(n, carry):
        strip = near_strip(n)

        @pl.when(n == 0)
        def _():
            got_coarse[strip] = coarse[pl.ds(pl.multiple_of(strip * 32, 32), 32), :]

        @pl.when(n > 0)
        def _():
            some = got_coarse.at[strip]
            pltpu.make_async_copy(some, some, coarse_in.at[strip]).wait()

        cells = got_coarse[strip].astype(F32)
        for q in range(4):
            for half in range(2):
                up[half, pl.ds(q, 32, stride=4), :] = cells[:, half * 128 : half * 128 + 128]

        def fine_row(q, carry):
            r = strip * 4 + q
            hidden = fine[r].astype(F32) + jnp.concatenate(
                [up[0, 0:COLS], up[1, 0:COLS]], axis=1
            )
            sig = 0.5 * jnp.tanh(0.5 * hidden) + 0.5
            value = hidden * sig
            at = pl.ds(pl.multiple_of(r * COLS, COLS), COLS)
            act[at, :] = value.astype(BF)
            slope[at, :] = sig + value * (1.0 - sig)
            return carry

        return lax.fori_loop(0, 4, fine_row, carry)

    lax.fori_loop(0, STRIPS, activate, 0)

    keep_top = jnp.where(row > 0, 1.0, 0.0)
    keep_bottom = jnp.where(row < 15, 1.0, 0.0)
    keep_left = jnp.where(col > 0, 1.0, 0.0)
    keep_right = jnp.where(col < 7, 1.0, 0.0)

    for copy in sent:
        copy.wait_recv()
    patch[0] = scaled(got_edge[0]).astype(F32) * keep_left
    patch[1] = scaled(got_edge[1]).astype(F32) * keep_right
    spot = lax.broadcasted_iota(jnp.int32, (16, C), 0)

    def patch_row(r, carry):
        first = pl.ds(pl.multiple_of((r + 1) * COLS, COLS), 16)
        last = pl.ds(pl.multiple_of((r + 1) * COLS + COLS - 16, 16), 16)
        lo = dcat[first, 2 * C : 3 * C].astype(F32)
        dcat[first, 2 * C : 3 * C] = jnp.where(spot == 0, patch[0, pl.ds(r, 1), :], lo).astype(BF)
        hi = dcat[last, 0:C].astype(F32)
        dcat[last, 0:C] = jnp.where(spot == 15, patch[1, pl.ds(r, 1), :], hi).astype(BF)
        return carry

    lax.fori_loop(0, ROWS, patch_row, 0)
    spot_row = lax.broadcasted_iota(jnp.int32, (COLS, C), 0)

    def outer_rows():
        for copy in outer:
            copy.wait_recv()
        for n, (start, keep) in enumerate(((0, keep_top), ((ROWS + 1) * COLS, keep_bottom))):
            wide = scaled(got_row[n]).astype(F32) * keep
            near = scaled(got_corner[2 * n]).astype(F32)[15:16] * (keep * keep_left)
            far = scaled(got_corner[2 * n + 1]).astype(F32)[0:1] * (keep * keep_right)
            at = pl.ds(start, COLS)
            dcat[at, C : 2 * C] = wide.astype(BF)
            dcat[at, 2 * C : 3 * C] = jnp.where(
                spot_row == 0, near, pltpu.roll(wide, 1, 0)
            ).astype(BF)
            dcat[at, 0:C] = jnp.where(
                spot_row == COLS - 1, far, pltpu.roll(wide, COLS - 1, 0)
            ).astype(BF)

    def mine(axis):
        return here[axis] * 2 + k

    def eight(axis):
        return [
            (((here[axis] + d) % 4) * 2 + (k + flip) % 2, other(axis, d, flip, *here))
            for d, flip in ((2, 1), (2, 0), (1, 1), (3, 1), (1, 0), (3, 0), (0, 1))
        ]

    def peers(axis):
        return [other(axis, d, 0, *here) for d in (2, 1, 3)]

    def arrived(some, sem):
        pltpu.make_async_copy(some, some, sem).wait()

    def total(stack, t):
        out = stack[t, 0].astype(F32)
        for n in range(1, stack.shape[1]):
            out = out + stack[t, n].astype(F32)
        return out.astype(BF)

    def quarter(m):
        return pl.ds(pl.multiple_of(m * PIECE, PIECE), PIECE)

    def three(stack, first, rows):
        return stack.at[pl.ds(first, 3), pl.ds(0, rows)]

    def exchange(before, after, phase):
        def step(g, first):
            arrived(three(before, first, before.shape[1] - 1), ar_in.at[phase - 1, g])
            for j in range(3):
                after[first + j, here[(j + phase) % 3]] = total(before, first + j)
            for n in range(3):
                for j in range(3):
                    t, axis = first + j, (j + phase) % 3
                    push(
                        after.at[t, here[axis]], after.at[t, here[axis]],
                        ar_out.at[phase], ar_in.at[phase, g], peers(axis)[n],
                    )

        return step

    def step3(g, first):
        arrived(three(stack3, first, 3), ar_in.at[2, g])
        for j in range(3):
            whole[first + j, quarter(mine(j)), :] = total(stack3, first + j)
        for n in range(7):
            for j in range(3):
                some = whole.at[first + j, quarter(mine(j))]
                push(some, some, ar_out.at[3], ar_in.at[3, g], eight(j)[n][1])

    scale = 1.0 / math.sqrt(PIX * GRID[0] * GRID[1])

    def step4(g, first):
        arrived(three(whole, first, 7 * PIECE), ar_in.at[3, g])
        for j in range(3):
            gw_ref[first + j] = whole[first + j].astype(F32) * scale

    def first_tap(g):
        return 3 * ((4 - g) % 3)

    def taps(g):
        first = first_tap(g)
        at = pl.ds(pl.multiple_of(2 * COLS - first // 3 * COLS, COLS), PIX)
        row_of_taps = lax.dot_general(act[...], dcat[at, :], TN, preferred_element_type=F32)
        for j in range(3):
            part[first + j] = row_of_taps[:, j * C : (j + 1) * C].astype(BF)
        for n in range(7):
            for j in range(3):
                t = first + j
                m, to = eight(j)[n]
                push(part.at[t, quarter(m)], stack1.at[t, mine(j)], ar_out.at[0], ar_in.at[0, g], to)
        for j in range(3):
            stack1[first + j, mine(j)] = part[first + j, quarter(mine(j)), :]

    def strip(n):
        c = (col + 1 + n) % 8
        base = c * (4 * COLS)
        acc = None
        for i in range(3):
            at = pl.ds(pl.multiple_of(base + (2 - i) * COLS, COLS), 4 * COLS)
            term = jnp.dot(dcat[at, :], wcat[i], preferred_element_type=F32)
            acc = term if acc is None else acc + term
        at = pl.ds(pl.multiple_of(base, COLS), 4 * COLS)
        dh = acc * slope[at, :]
        gf_ref[at, :] = dh.astype(BF)
        tall = dh[0:COLS] + dh[COLS : 2 * COLS] + dh[2 * COLS : 3 * COLS] + dh[3 * COLS :]
        for half in range(2):
            lanes = slice(half * 128, half * 128 + 128)
            pooled_rows[half, 0:COLS] = tall[:, lanes]
            cells = pooled_rows[half, pl.ds(0, 32, stride=4), :]
            for q in range(1, 4):
                cells = cells + pooled_rows[half, pl.ds(q, 32, stride=4), :]
            pool[n, :, lanes] = cells.astype(BF)
        slot = pl.ds(pl.multiple_of(col * 32, 32), 32)

        @pl.when(n < 7)
        def _():
            push(pool.at[n], got_pool.at[slot], pool_out, pool_in, (row, c))

        @pl.when(n == 7)
        def _():
            got_pool[slot, :] = pool[n]

    steps = (exchange(stack1, stack2, 1), exchange(stack2, stack3, 2), step3, step4)

    def slot(u, carry):
        @pl.when(u == 1)
        def _():
            outer_rows()

        @pl.when(u < 3)
        def _():
            taps(u)

        @pl.when((u >= 3) & (u < 3 + STRIPS))
        def _():
            strip(u - 3)

        for step, (first, second, third) in zip(steps, WHEN):
            @pl.when((u == first) | (u == second) | (u == third))
            def _():
                g = jnp.where(u == first, 0, jnp.where(u == second, 1, 2))
                step(g, first_tap(g))

        return carry

    lax.fori_loop(0, WHEN[-1][-1], slot, 0)

    arrived(got_pool.at[pl.ds(0, 7 * 32)], pool_in)
    gc_ref[...] = got_pool[...]
    arrived(pool.at[pl.ds(0, 7)], pool_out)
    for copy in sent + outer:
        copy.wait_send()
    arrived(got_coarse.at[pl.ds(0, 7)], coarse_out)
    for phase, count in enumerate((7, 3, 3, 7)):
        arrived(dcat.at[pl.ds(0, 9 * count * PIECE // 3)], ar_out.at[phase])
    steps[-1](2, first_tap(2))


def store_kernel(gf_ref, gc_ref, gw_ref, gf_out, gc_out, gw_out, sem):
    pairs = [(gw_ref.at[t], gw_out.at[t]) for t in range(9)]
    for n in range(8):
        some = pl.ds(n * (PIX // 8), PIX // 8)
        pairs.append((gf_ref.at[some], gf_out.at[some]))
    pairs.append((gc_ref, gc_out))
    copies = [pltpu.make_async_copy(*pair, sem.at[n]) for n, pair in enumerate(pairs)]
    for copy in copies:
        copy.start()
    for copy in copies:
        copy.wait()


def per_device(fine_input, coarse_feat, conv_weight, step_scale, timesteps, cotangent):
    anywhere = pl.BlockSpec(memory_space=pl.ANY)
    vmem = pl.BlockSpec(memory_space=pltpu.VMEM)
    buf = pltpu.VMEM
    dma = pltpu.SemaphoreType.DMA
    def in_hbm(array, shape):
        return pltpu.with_memory_space_constraint(array.reshape(shape), pltpu.HBM)

    results = pl.pallas_call(
        fused_kernel,
        name="fused",
        out_shape=(
            pltpu.VMEM((PIX, C), BF),
            pltpu.VMEM((C, C), BF),
            pltpu.VMEM((9, C, C), F32),
        ),
        in_specs=[pl.BlockSpec(memory_space=pltpu.SMEM)] + [anywhere] * 5,
        out_specs=(vmem, vmem, vmem),
        scratch_shapes=[
            buf((1000, C), F32),
            buf((ROWS, COLS, C), BF),
            buf((ROWS, COLS, C), BF),
            buf((C, C), BF),
            buf((9, C, C), BF),
            buf((3, 3 * C, C), BF),
            buf(((ROWS + 2) * COLS, 3 * C), BF),
            buf((PIX, C), BF),
            buf((PIX, C), F32),
            buf((2, ROWS, 16, C), BF),
            buf((2, ROWS, C), F32),
            buf((2, ROWS, C), BF),
            buf((2, ROWS, C), BF),
            buf((2, COLS, C), BF),
            buf((4, 16, C), BF),
            buf((8, 32, C), BF),
            buf((2, COLS + 8, 128), F32),
            buf((2, ROWS, C), F32),
            buf((8, 32, C), BF),
            buf((C, C), BF),
            buf((9, C, C), BF),
            buf((9, 8, PIECE, C), BF),
            buf((9, 4, PIECE, C), BF),
            buf((9, 4, PIECE, C), BF),
            buf((9, C, C), BF),
            buf((2, COLS + 8, 128), F32),
            dma((7,)),
            dma((8,)),
            dma((8,)),
            dma,
            dma((8,)),
            dma,
            dma,
            dma((4,)),
            dma((4, 3)),
        ],
        compiler_params=pltpu.CompilerParams(
            collective_id=0, has_side_effects=True, vmem_limit_bytes=40 * 2**20
        ),
        cost_estimate=pl.CostEstimate(
            flops=2 * 2 * 9 * PIX * C * C, bytes_accessed=12 * 2**20, transcendentals=PIX * C
        ),
    )(
        timesteps,
        in_hbm(step_scale, step_scale.shape),
        in_hbm(fine_input, (ROWS, COLS, C)),
        in_hbm(coarse_feat, (C, C)),
        in_hbm(conv_weight, (9, C, C)),
        in_hbm(cotangent, (ROWS, COLS, C)),
    )
    gf, gc, gw = pl.pallas_call(
        store_kernel,
        name="store",
        out_shape=(
            jax.ShapeDtypeStruct((PIX, C), BF),
            jax.ShapeDtypeStruct((C, C), BF),
            jax.ShapeDtypeStruct((9, C, C), F32),
        ),
        in_specs=[vmem] * 3,
        out_specs=(anywhere, anywhere, anywhere),
        scratch_shapes=[dma((18,))],
        compiler_params=pltpu.CompilerParams(vmem_limit_bytes=2**20),
    )(*(pltpu.with_memory_space_constraint(result, pltpu.VMEM) for result in results))
    return gf.reshape(1, ROWS, COLS, C), gc.reshape(1, 1, C, C), gw.reshape(3, 3, C, C)


def solution(mesh):
    return jax.shard_map(
        per_device,
        mesh=mesh,
        in_specs=(
            P(None, "row", "col", None),
            P(None, ("row", "col"), None, None),
            P(),
            P(),
            P(),
            P(None, "row", "col", None),
        ),
        out_specs=(P(None, "row", "col", None), P(None, ("row", "col"), None, None), P()),
        check_vma=False,
    )
```

```python
import functools
import math

import jax
import jax.numpy as jnp
from jax import lax
from jax.experimental import pallas as pl
from jax.experimental.pallas import tpu as pltpu
from jax.sharding import PartitionSpec as P

MESH = pl.DeviceIdType.MESH
BF = jnp.bfloat16
F32 = jnp.float32
TN = (((0,), (0,)), ((), ()))
ROWS, COLS, C = 32, 128, 256
PIX = ROWS * COLS
GRID = (16, 8)
STRIPS = 8
PIECE = C // 8
WHEN = ((3, 4, 5), (6, 7, 8), (8, 9, 11), (12, 13, 14))


def place(x, y, z, k):
    return (y * 4 + (z // 2) * 2 + k, (z % 2) * 4 + x)


def other(axis, d, flip, x, y, z, k):
    at = [x, y, z]
    at[axis] = (at[axis] + d) % 4
    return place(*at, (k + flip) % 2)


def fused_kernel(
    ts, ss_hbm, fine_hbm, coarse_hbm, w_hbm, cot_hbm,
    gf_ref, gc_ref, gw_ref,
    ss, cot, fine, coarse, w, wcat, dcat, act,
    rim, edge32, edge, got_edge, got_row, got_corner, got_coarse, up, patch,
    pool, got_pool, part, stack1, stack2, stack3, whole, pooled_rows,
    load_sem, out_sem, in_sem, coarse_out, coarse_in, pool_out, pool_in, ar_out, ar_in,
):
    row, col = lax.axis_index("row"), lax.axis_index("col")
    y, z_hi, k, z_lo, x = row // 4, (row // 2) % 2, row % 2, col // 4, col % 4
    z = z_hi * 2 + z_lo
    here = (x, y, z, k)

    down, upw, right, left = (row + 1) % 16, (row + 15) % 16, (col + 1) % 8, (col + 7) % 8
    partners = [(row, (col + d) % 8) for d in range(1, 8)]
    partners += [(down, col), (upw, col)]
    partners += [(a, b) for a in (down, upw) for b in (left, right)]
    partners += [other(1, d, 0, *here) for d in range(1, 4)]
    partners += [place(x, y, (z + 2) % 4, k), place(x, y, 3 - z, k)]
    partners += [other(axis, d, 1, *here) for axis in range(3) for d in range(1, 4)]
    barrier = pltpu.get_barrier_semaphore()
    for partner in partners:
        pl.semaphore_signal(barrier, inc=1, device_id=partner, device_id_type=MESH)

    loads = [
        pltpu.make_async_copy(src, dst, load_sem.at[n])
        for n, (src, dst) in enumerate(
            (
                (coarse_hbm, coarse), (cot_hbm.at[:, pl.ds(0, 16)], rim.at[0]),
                (cot_hbm.at[:, pl.ds(COLS - 16, 16)], rim.at[1]), (cot_hbm, cot),
                (ss_hbm, ss), (w_hbm, w), (fine_hbm, fine),
            )
        )
    ]
    for copy in loads[:4]:
        copy.start()

    def push(src, dst, send, recv, to):
        copy = pltpu.make_async_remote_copy(
            src_ref=src, dst_ref=dst, send_sem=send, recv_sem=recv,
            device_id=to, device_id_type=MESH,
        )
        copy.start()
        return copy

    def near_strip(n):
        m = n % 4
        return ((z_lo + n // 4) % 2) * 4 + (x + (m * (m + 1) // 2)) % 4

    loads[0].wait()
    pl.semaphore_wait(barrier, len(partners))
    for n in range(7, 0, -1):
        to = near_strip(n)
        push(
            coarse.at[pl.ds(pl.multiple_of(to * 32, 32), 32)], got_coarse.at[col],
            coarse_out, coarse_in.at[col], (row, to),
        )

    for copy in loads[4:]:
        copy.start()

    loads[1].wait()
    loads[2].wait()

    outer = []
    for n, (side, src_row, to) in enumerate(
        (
            (1, ROWS - 1, (down, right)),
            (0, ROWS - 1, (down, left)),
            (1, 0, (upw, right)),
            (0, 0, (upw, left)),
        )
    ):
        outer.append(
            push(
                rim.at[side, src_row], got_corner.at[n],
                out_sem.at[4 + n], in_sem.at[4 + n], to,
            )
        )

    outer.append(push(cot_hbm.at[ROWS - 1], got_row.at[0], out_sem.at[2], in_sem.at[2], (down, col)))
    outer.append(push(cot_hbm.at[0], got_row.at[1], out_sem.at[3], in_sem.at[3], (upw, col)))

    def take_edge(r, carry):
        edge32[0, pl.ds(r, 1), :] = rim[0, r].astype(F32)[0:1]
        edge32[1, pl.ds(r, 1), :] = rim[1, r].astype(F32)[15:16]
        return carry

    lax.fori_loop(0, ROWS, take_edge, 0)
    edge[...] = edge32[...].astype(BF)
    sent = [
        push(edge.at[1], got_edge.at[0], out_sem.at[0], in_sem.at[0], (row, right)),
        push(edge.at[0], got_edge.at[1], out_sem.at[1], in_sem.at[1], (row, left)),
    ]
    loads[3].wait()

    loads[4].wait()
    picked = ss[pl.ds(ts[0], 1), :]

    def scaled(raw):
        return (raw.astype(F32) * picked).astype(BF)

    def shift_row(r, carry):
        mid = scaled(cot[r])
        wide = mid.astype(F32)
        at = pl.ds(pl.multiple_of((r + 1) * COLS, COLS), COLS)
        dcat[at, C : 2 * C] = mid
        dcat[at, 2 * C : 3 * C] = pltpu.roll(wide, 1, 0).astype(BF)
        dcat[at, 0:C] = pltpu.roll(wide, COLS - 1, 0).astype(BF)
        return carry

    lax.fori_loop(0, ROWS, shift_row, 0)

    loads[5].wait()

    def turn_weight(i, carry):
        for j in range(3):
            wcat[i, j * C : (j + 1) * C, :] = w[3 * i + j].T
        return carry

    lax.fori_loop(0, 3, turn_weight, 0)

    loads[6].wait()

    def activate(n, carry):
        strip = near_strip(n)

        @pl.when(n == 0)
        def _():
            got_coarse[strip] = coarse[pl.ds(pl.multiple_of(strip * 32, 32), 32), :]

        @pl.when(n > 0)
        def _():
            some = got_coarse.at[strip]
            pltpu.make_async_copy(some, some, coarse_in.at[strip]).wait()

        cells = got_coarse[strip].astype(F32)
        for q in range(4):
            for half in range(2):
                up[half, pl.ds(q, 32, stride=4), :] = cells[:, half * 128 : half * 128 + 128]

        def fine_row(q, carry):
            r = strip * 4 + q
            hidden = fine[r].astype(F32) + jnp.concatenate(
                [up[0, 0:COLS], up[1, 0:COLS]], axis=1
            )
            sig = 0.5 * jnp.tanh(0.5 * hidden) + 0.5
            value = hidden * sig
            at = pl.ds(pl.multiple_of(r * COLS, COLS), COLS)
            act[at, :] = value.astype(BF)
            return carry

        return lax.fori_loop(0, 4, fine_row, carry)

    lax.fori_loop(0, STRIPS, activate, 0)

    keep_top = jnp.where(row > 0, 1.0, 0.0)
    keep_bottom = jnp.where(row < 15, 1.0, 0.0)
    keep_left = jnp.where(col > 0, 1.0, 0.0)
    keep_right = jnp.where(col < 7, 1.0, 0.0)

    for copy in sent:
        copy.wait_recv()
    patch[0] = scaled(got_edge[0]).astype(F32) * keep_left
    patch[1] = scaled(got_edge[1]).astype(F32) * keep_right
    spot = lax.broadcasted_iota(jnp.int32, (16, C), 0)

    def patch_row(r, carry):
        first = pl.ds(pl.multiple_of((r + 1) * COLS, COLS), 16)
        last = pl.ds(pl.multiple_of((r + 1) * COLS + COLS - 16, 16), 16)
        lo = dcat[first, 2 * C : 3 * C].astype(F32)
        dcat[first, 2 * C : 3 * C] = jnp.where(spot == 0, patch[0, pl.ds(r, 1), :], lo).astype(BF)
        hi = dcat[last, 0:C].astype(F32)
        dcat[last, 0:C] = jnp.where(spot == 15, patch[1, pl.ds(r, 1), :], hi).astype(BF)
        return carry

    lax.fori_loop(0, ROWS, patch_row, 0)
    spot_row = lax.broadcasted_iota(jnp.int32, (COLS, C), 0)

    def outer_rows():
        for copy in outer:
            copy.wait_recv()
        for n, (start, keep) in enumerate(((0, keep_top), ((ROWS + 1) * COLS, keep_bottom))):
            wide = scaled(got_row[n]).astype(F32) * keep
            near = scaled(got_corner[2 * n]).astype(F32)[15:16] * (keep * keep_left)
            far = scaled(got_corner[2 * n + 1]).astype(F32)[0:1] * (keep * keep_right)
            at = pl.ds(start, COLS)
            dcat[at, C : 2 * C] = wide.astype(BF)
            dcat[at, 2 * C : 3 * C] = jnp.where(
                spot_row == 0, near, pltpu.roll(wide, 1, 0)
            ).astype(BF)
            dcat[at, 0:C] = jnp.where(
                spot_row == COLS - 1, far, pltpu.roll(wide, COLS - 1, 0)
            ).astype(BF)

    def mine(axis):
        return here[axis] * 2 + k

    def eight(axis):
        return [
            (((here[axis] + d) % 4) * 2 + (k + flip) % 2, other(axis, d, flip, *here))
            for d, flip in ((2, 1), (2, 0), (1, 1), (3, 1), (1, 0), (3, 0), (0, 1))
        ]

    def peers(axis):
        return [other(axis, d, 0, *here) for d in (2, 1, 3)]

    def arrived(some, sem):
        pltpu.make_async_copy(some, some, sem).wait()

    def total(stack, t):
        out = stack[t, 0].astype(F32)
        for n in range(1, stack.shape[1]):
            out = out + stack[t, n].astype(F32)
        return out.astype(BF)

    def quarter(m):
        return pl.ds(pl.multiple_of(m * PIECE, PIECE), PIECE)

    def three(stack, first, rows):
        return stack.at[pl.ds(first, 3), pl.ds(0, rows)]

    def exchange(before, after, phase):
        def step(g, first):
            arrived(three(before, first, before.shape[1] - 1), ar_in.at[phase - 1, g])
            for j in range(3):
                after[first + j, here[(j + phase) % 3]] = total(before, first + j)
            for n in range(3):
                for j in range(3):
                    t, axis = first + j, (j + phase) % 3
                    push(
                        after.at[t, here[axis]], after.at[t, here[axis]],
                        ar_out.at[phase], ar_in.at[phase, g], peers(axis)[n],
                    )

        return step

    def step3(g, first):
        arrived(three(stack3, first, 3), ar_in.at[2, g])
        for j in range(3):
            whole[first + j, quarter(mine(j)), :] = total(stack3, first + j)
        for n in range(7):
            for j in range(3):
                some = whole.at[first + j, quarter(mine(j))]
                push(some, some, ar_out.at[3], ar_in.at[3, g], eight(j)[n][1])

    scale = 1.0 / math.sqrt(PIX * GRID[0] * GRID[1])

    def step4(g, first):
        arrived(three(whole, first, 7 * PIECE), ar_in.at[3, g])
        for j in range(3):
            gw_ref[first + j] = whole[first + j].astype(F32) * scale

    def first_tap(g):
        return 3 * ((4 - g) % 3)

    def taps(g):
        first = first_tap(g)
        at = pl.ds(pl.multiple_of(2 * COLS - first // 3 * COLS, COLS), PIX)
        row_of_taps = lax.dot_general(act[...], dcat[at, :], TN, preferred_element_type=F32)
        for j in range(3):
            part[first + j] = row_of_taps[:, j * C : (j + 1) * C].astype(BF)
        for n in range(7):
            for j in range(3):
                t = first + j
                m, to = eight(j)[n]
                push(part.at[t, quarter(m)], stack1.at[t, mine(j)], ar_out.at[0], ar_in.at[0, g], to)
        for j in range(3):
            stack1[first + j, mine(j)] = part[first + j, quarter(mine(j)), :]

    def strip(n):
        c = (col + 1 + n) % 8
        base = c * (4 * COLS)
        acc = None
        for i in range(3):
            at = pl.ds(pl.multiple_of(base + (2 - i) * COLS, COLS), 4 * COLS)
            term = jnp.dot(dcat[at, :], wcat[i], preferred_element_type=F32)
            acc = term if acc is None else acc + term
        at = pl.ds(pl.multiple_of(base, COLS), 4 * COLS)
        cells = got_coarse[c].astype(F32)
        for q in range(4):
            for half in range(2):
                up[half, pl.ds(q, 32, stride=4), :] = cells[:, half * 128 : half * 128 + 128]
        upper = jnp.concatenate([up[0, 0:COLS], up[1, 0:COLS]], axis=1)
        slopes = []
        for q in range(4):
            hidden = fine[c * 4 + q].astype(F32) + upper
            sig = 0.5 * jnp.tanh(0.5 * hidden) + 0.5
            slopes.append(sig + hidden * sig * (1.0 - sig))
        dh = acc * jnp.concatenate(slopes, axis=0)
        gf_ref[at, :] = dh.astype(BF)
        tall = dh[0:COLS] + dh[COLS : 2 * COLS] + dh[2 * COLS : 3 * COLS] + dh[3 * COLS :]
        for half in range(2):
            lanes = slice(half * 128, half * 128 + 128)
            pooled_rows[half, 0:COLS] = tall[:, lanes]
            cells = pooled_rows[half, pl.ds(0, 32, stride=4), :]
            for q in range(1, 4):
                cells = cells + pooled_rows[half, pl.ds(q, 32, stride=4), :]
            pool[n, :, lanes] = cells.astype(BF)
        slot = pl.ds(pl.multiple_of(col * 32, 32), 32)

        @pl.when(n < 7)
        def _():
            push(pool.at[n], got_pool.at[slot], pool_out, pool_in, (row, c))

        @pl.when(n == 7)
        def _():
            got_pool[slot, :] = pool[n]

    steps = (exchange(stack1, stack2, 1), exchange(stack2, stack3, 2), step3, step4)

    def slot(u, carry):
        @pl.when(u == 1)
        def _():
            outer_rows()

        @pl.when(u < 3)
        def _():
            taps(u)

        @pl.when((u >= 3) & (u < 3 + STRIPS))
        def _():
            strip(u - 3)

        for step, (first, second, third) in zip(steps, WHEN):
            @pl.when((u == first) | (u == second) | (u == third))
            def _():
                g = jnp.where(u == first, 0, jnp.where(u == second, 1, 2))
                step(g, first_tap(g))

        return carry

    lax.fori_loop(0, WHEN[-1][-1], slot, 0)

    arrived(got_pool.at[pl.ds(0, 7 * 32)], pool_in)
    gc_ref[...] = got_pool[...]
    arrived(pool.at[pl.ds(0, 7)], pool_out)
    for copy in sent + outer:
        copy.wait_send()
    arrived(got_coarse.at[pl.ds(0, 7)], coarse_out)
    for phase, count in enumerate((7, 3, 3, 7)):
        arrived(dcat.at[pl.ds(0, 9 * count * PIECE // 3)], ar_out.at[phase])
    steps[-1](2, first_tap(2))


def store_kernel(gf_ref, gc_ref, gw_ref, gf_out, gc_out, gw_out, sem):
    pairs = [(gw_ref.at[t], gw_out.at[t]) for t in range(9)]
    for n in range(4):
        some = pl.ds(n * (PIX // 4), PIX // 4)
        pairs.append((gf_ref.at[some], gf_out.at[some]))
    pairs.append((gc_ref, gc_out))
    copies = [pltpu.make_async_copy(*pair, sem.at[n]) for n, pair in enumerate(pairs)]
    for copy in copies:
        copy.start()
    for copy in copies:
        copy.wait()


def per_device(fine_input, coarse_feat, conv_weight, step_scale, timesteps, cotangent):
    anywhere = pl.BlockSpec(memory_space=pl.ANY)
    vmem = pl.BlockSpec(memory_space=pltpu.VMEM)
    buf = pltpu.VMEM
    dma = pltpu.SemaphoreType.DMA
    def in_hbm(array, shape):
        return pltpu.with_memory_space_constraint(array.reshape(shape), pltpu.HBM)

    results = pl.pallas_call(
        fused_kernel,
        name="fused",
        out_shape=(
            pltpu.VMEM((PIX, C), BF),
            pltpu.VMEM((C, C), BF),
            pltpu.VMEM((9, C, C), F32),
        ),
        in_specs=[pl.BlockSpec(memory_space=pltpu.SMEM)] + [anywhere] * 5,
        out_specs=(vmem, vmem, vmem),
        scratch_shapes=[
            buf((1000, C), F32),
            buf((ROWS, COLS, C), BF),
            buf((ROWS, COLS, C), BF),
            buf((C, C), BF),
            buf((9, C, C), BF),
            buf((3, 3 * C, C), BF),
            buf(((ROWS + 2) * COLS, 3 * C), BF),
            buf((PIX, C), BF),
            buf((2, ROWS, 16, C), BF),
            buf((2, ROWS, C), F32),
            buf((2, ROWS, C), BF),
            buf((2, ROWS, C), BF),
            buf((2, COLS, C), BF),
            buf((4, 16, C), BF),
            buf((8, 32, C), BF),
            buf((2, COLS + 8, 128), F32),
            buf((2, ROWS, C), F32),
            buf((8, 32, C), BF),
            buf((C, C), BF),
            buf((9, C, C), BF),
            buf((9, 8, PIECE, C), BF),
            buf((9, 4, PIECE, C), BF),
            buf((9, 4, PIECE, C), BF),
            buf((9, C, C), BF),
            buf((2, COLS + 8, 128), F32),
            dma((7,)),
            dma((8,)),
            dma((8,)),
            dma,
            dma((8,)),
            dma,
            dma,
            dma((4,)),
            dma((4, 3)),
        ],
        compiler_params=pltpu.CompilerParams(
            collective_id=0, has_side_effects=True, vmem_limit_bytes=40 * 2**20
        ),
        cost_estimate=pl.CostEstimate(
            flops=2 * 2 * 9 * PIX * C * C, bytes_accessed=12 * 2**20, transcendentals=PIX * C
        ),
    )(
        timesteps,
        in_hbm(step_scale, step_scale.shape),
        in_hbm(fine_input, (ROWS, COLS, C)),
        in_hbm(coarse_feat, (C, C)),
        in_hbm(conv_weight, (9, C, C)),
        in_hbm(cotangent, (ROWS, COLS, C)),
    )
    gf, gc, gw = pl.pallas_call(
        store_kernel,
        name="store",
        out_shape=(
            jax.ShapeDtypeStruct((PIX, C), BF),
            jax.ShapeDtypeStruct((C, C), BF),
            jax.ShapeDtypeStruct((9, C, C), F32),
        ),
        in_specs=[vmem] * 3,
        out_specs=(anywhere, anywhere, anywhere),
        scratch_shapes=[dma((14,))],
        compiler_params=pltpu.CompilerParams(vmem_limit_bytes=2**20),
    )(*(pltpu.with_memory_space_constraint(result, pltpu.VMEM) for result in results))
    return gf.reshape(1, ROWS, COLS, C), gc.reshape(1, 1, C, C), gw.reshape(3, 3, C, C)


def solution(mesh):
    return jax.shard_map(
        per_device,
        mesh=mesh,
        in_specs=(
            P(None, "row", "col", None),
            P(None, ("row", "col"), None, None),
            P(),
            P(),
            P(),
            P(None, "row", "col", None),
        ),
        out_specs=(P(None, "row", "col", None), P(None, ("row", "col"), None, None), P()),
        check_vma=False,
    )
```
